32 devices in a mesh: req: 8 (over y, x, core), mlp: 4 (over z).
Axes of the slice: x: 2, y: 2, z: 4, core: 2. Of those that a mesh axis runs over, the one named last changes fastest.
Arguments:
- hidden_in: bfloat16 [16, 512, 2048], P('req'), may hold values from -6 to 6
- lengths: int32 [16], replicated, may hold values from 1 to 512, 4096 in all
- slot_request: int32 [16], replicated, may hold values from 0 to 15, each once
- adapter_of: int32 [16], replicated, may hold values from 0 to 63, as said below
- adapter_slot: int32 [64], replicated, may hold values from 0 to 63, each once
- norm_gain_attn: float32 [2048], replicated, may hold values from 0.5 to 1.5
- norm_gain_mlp: float32 [2048], replicated, may hold values from 0.5 to 1.5
- final_gain: float32 [2048], replicated, may hold values from 0.5 to 1.5
- w_qkv: bfloat16 [2048, 3, 2048], P(None, None, 'mlp')
- w_out: bfloat16 [2048, 2048], P('mlp'), may hold values from -0.125 to 0.125
- w_gateup: bfloat16 [2048, 2, 4096], P('req', None, 'mlp'), may hold values from -0.125 to 0.125
- w_down: bfloat16 [4096, 2048], P('mlp', 'req'), may hold values from -0.09375 to 0.09375
- adapter_down: bfloat16 [64, 16, 2048], P('req'), may hold values from -0.125 to 0.125
- adapter_up: bfloat16 [64, 16, 2048], P('req', None, 'mlp'), may hold values from -1.5 to 1.5
- vocab: bfloat16 [49152, 2048], P(('req', 'mlp')), may hold values from -0.375 to 0.375
Outputs:
- out_hidden: bfloat16 [16, 512, 2048], P('req')
- request_norm: float32 [16], replicated
- request_peak: float32 [16], replicated
The draws below stay inside these ranges and needn't reach their ends.
Inputs may be any that keep to these rules, and one draw needn't show every extreme that they name: Some request has exactly 512 tokens, and all lengths together sum to 4096. `slot_request`: each request sits in exactly one slot. `adapter_of`: exactly 16 distinct adapters are named. `adapter_slot`: each adapter sits in exactly one row of the adapter tables.
All inputs are finite; a program needn't handle non-finite values.
Results may differ from the reference program's by a relative error of at most 0.018.
Values may be sent and summed in bfloat16 or wider, within the bound.
No kernel may reach another device: no remote copies, remote signals or barrier semaphores. Data moves between devices by JAX's collectives and lax.ppermute only.
A program may use at most 128 MiB of HBM per device.

```python
import math
import jax
import jax.numpy as jnp
import numpy as np
from jax import lax

D = 2048
ATTENTION_HEADS = 32
HEAD_WIDTH = 64
FF = 4096
VOCAB = 49152
ADAPTERS = 64
ACTIVE = 16
RANK = 16
TOKEN_SLOTS = 512
R = 16
N_MLP = 4


def draw_adapter_of(key, part):
    key_one, key_two, key_three, key_four = jax.random.split(key, 4)
    chosen = jax.random.permutation(key_one, ADAPTERS)[:ACTIVE]
    order = jax.random.permutation(key_two, R)
    first_draw = jax.random.randint(key_three, (R,), 0, ACTIVE)
    second_draw = jax.random.randint(key_four, (R,), 0, ACTIVE)
    skewed = first_draw * second_draw // ACTIVE
    choose_index = jnp.where(order < ACTIVE, order, skewed)
    return jnp.take(chosen, choose_index).astype(jnp.int32)


def draw_w_qkv(key, part):
    own_key = jax.random.fold_in(key, 7013)
    key_base, key_heads, key_strength = jax.random.split(own_key, 3)
    base = jnp.clip(jax.random.normal(key_base, (D, 3, D), jnp.float32), -6.0, 6.0) * D ** (-0.5)
    strong_count = max(1, ATTENTION_HEADS // 8)
    head_order = jax.random.permutation(key_heads, ATTENTION_HEADS)
    strong_heads = head_order < strong_count
    strength = jax.random.uniform(key_strength, (ATTENTION_HEADS,), jnp.float32, 150.0, 400.0) * HEAD_WIDTH ** (-0.5)
    strong_columns = jnp.repeat(strong_heads, HEAD_WIDTH)
    factor_columns = jnp.repeat(strength, HEAD_WIDTH)
    query_part = base[:, 0, :]
    key_part = jnp.where(strong_columns[None, :], query_part * factor_columns[None, :], base[:, 1, :])
    joined = jnp.stack([query_part, key_part, base[:, 2, :]], axis=1)
    return joined.astype(jnp.bfloat16)


def block_levels(stream_key, extent, shards, least, high):
    factor_of = 1.0
    for axis_at, parts in shards:
        steps = jax.random.uniform(jax.random.fold_in(jax.random.fold_in(stream_key, 6), axis_at), (parts,), jnp.float32, least / len(shards), high / len(shards))
        factor_of = factor_of * jnp.repeat(jnp.exp(steps), extent[axis_at] // parts).reshape((-1,) + (1,) * (len(extent) - 1 - axis_at))
    return factor_of


def split_up(number_of, total, most, slope):
    portions = [(1 << 20) // math.isqrt(standing ** slope) + 1 for standing in range(2, number_of + 1)]
    spare, given = total - most - (number_of - 1), [1] * (number_of - 1)
    while spare > 0:
        free = [i for i in range(number_of - 1) if given[i] < most]
        pool, budget = sum([portions[i] for i in free]), spare
        for i in free:
            addition = min(most - given[i], max(1, budget * portions[i] // pool), spare)
            given[i] = given[i] + addition
            spare = spare - addition
    return np.array([most] + given)


def ragged_sizes(key, amount, total, limit, skew):
    if amount == 2:
        one = jax.random.randint(key, (), max(1, total - limit), min(limit, total - 1) + 1)
        return jnp.stack([one, total - one])
    tallies = jnp.asarray(split_up(amount, total, limit, skew), jnp.int32)
    couples = (amount - 1) // 2
    giver, taker = tallies[1:1 + 2 * couples:2], tallies[2:2 + 2 * couples:2]
    margin = jnp.minimum(giver - 1, limit - taker)
    moved = jax.random.randint(jax.random.fold_in(key, 1), (couples,), 0, 1 << 20) % (margin + 1)
    tallies = tallies.at[1:1 + 2 * couples:2].set(giver - moved).at[2:2 + 2 * couples:2].set(taker + moved)
    return tallies[jax.random.permutation(jax.random.fold_in(key, 2), amount)]


def normal_values(rng, dims, scale, bound, cuts=(), kind=jnp.bfloat16):
    array = scale * jax.random.normal(rng, dims, jnp.float32)
    if cuts:
        array = array * block_levels(rng, dims, cuts, -0.22, 0.18)
    return jnp.clip(array, -bound, bound).astype(kind)


def setup_inputs(seed: int = 0) -> dict:
    key_list = jax.random.split(jax.random.key(seed), 16)
    hidden_in = normal_values(key_list[0], (R, TOKEN_SLOTS, D), 1.0, 6.0, ((0, 8),))
    lengths = ragged_sizes(key_list[1], R, R * TOKEN_SLOTS // 2, TOKEN_SLOTS, 2).astype(jnp.int32)
    slot_request = jax.random.permutation(key_list[2], R).astype(jnp.int32)
    adapter_of = draw_adapter_of(jax.random.fold_in(key_list[15], 71), 0)
    adapter_slot = jax.random.permutation(key_list[4], ADAPTERS).astype(jnp.int32)
    norm_gain_attn = jnp.clip(1.0 + 0.1 * jax.random.normal(key_list[5], (D,), jnp.float32), 0.5, 1.5)
    norm_gain_mlp = jnp.clip(1.0 + 0.1 * jax.random.normal(key_list[6], (D,), jnp.float32), 0.5, 1.5)
    final_gain = jnp.clip(1.0 + 0.1 * jax.random.normal(key_list[7], (D,), jnp.float32), 0.5, 1.5)
    w_qkv = draw_w_qkv(jax.random.fold_in(key_list[15], 71), 0)
    w_out = normal_values(key_list[9], (D, D), D ** -0.5, 0.125, ((0, 4),))
    w_gateup = normal_values(key_list[10], (D, 2, FF), D ** -0.5, 0.125, ((0, 8), (2, 4)))
    w_down = normal_values(key_list[11], (FF, D), FF ** -0.5, 0.09375, ((0, 4), (1, 8)))
    adapter_down = normal_values(key_list[12], (ADAPTERS, RANK, D), D ** -0.5, 0.125, ((0, 8),))
    adapter_up = normal_values(key_list[13], (ADAPTERS, RANK, D), RANK ** -0.5, 1.5, ((0, 8), (2, 4)))
    vocab = normal_values(key_list[14], (VOCAB, D), (D // 9) ** -0.5, 0.375, ((0, 32),))
    return dict(hidden_in=hidden_in, lengths=lengths, slot_request=slot_request, adapter_of=adapter_of, adapter_slot=adapter_slot, norm_gain_attn=norm_gain_attn, norm_gain_mlp=norm_gain_mlp, final_gain=final_gain, w_qkv=w_qkv, w_out=w_out, w_gateup=w_gateup, w_down=w_down, adapter_down=adapter_down, adapter_up=adapter_up, vocab=vocab)


EPSILON = 1e-05
ROPE_BASE = 130000.0
ADAPTER_SCALE = 2.0
MASKED = -1e+30

def rms_norm(values, gain):
    return values * lax.rsqrt(lax.optimization_barrier(jnp.mean(values * values, axis=-1, keepdims=True)) + EPSILON) * gain

def rotary_embedded(tensor):
    length = tensor.shape[-3]
    half_width = tensor.shape[-1] // 2
    frequency = ROPE_BASE ** (-(jnp.arange(half_width, dtype=jnp.float32) * 2.0 / tensor.shape[-1]))
    angles = jnp.arange(length, dtype=jnp.float32)[:, None] * frequency[None, :]
    cosine = jnp.cos(angles)[:, None, :]
    sine_part = jnp.sin(angles)[:, None, :]
    front_half = tensor[..., :half_width]
    back_half = tensor[..., half_width:]
    return jnp.concatenate([front_half * cosine - back_half * sine_part, back_half * cosine + front_half * sine_part], axis=-1)

def reference(hidden_in, lengths, slot_request, adapter_of, adapter_slot, norm_gain_attn, norm_gain_mlp, final_gain, w_qkv, w_out, w_gateup, w_down, adapter_down, adapter_up, vocab):
    slot_lengths = jnp.take(lengths, slot_request)
    slot_tables = jnp.take(adapter_slot, jnp.take(adapter_of, slot_request))
    positions = jnp.arange(TOKEN_SLOTS)
    group_heads = D // N_MLP
    group_units = FF // N_MLP

    def one_slot(slot_items):
        hidden, length, table_row = slot_items
        residual_in = hidden.astype(jnp.float32)
        normed = rms_norm(residual_in, norm_gain_attn).astype(jnp.bfloat16)
        projected_rows = jnp.dot(normed, w_qkv.reshape(D, 3 * D), preferred_element_type=jnp.float32).reshape(TOKEN_SLOTS, 3, D)
        down_one = lax.dynamic_index_in_dim(adapter_down, table_row, 0, keepdims=False)
        up_one = lax.dynamic_index_in_dim(adapter_up, table_row, 0, keepdims=False)
        low_rank = jnp.dot(normed, down_one.T, preferred_element_type=jnp.float32).astype(jnp.bfloat16)
        raised_rows = jnp.dot(low_rank, up_one, preferred_element_type=jnp.float32)
        query_head_rows = rotary_embedded((projected_rows[:, 0] + ADAPTER_SCALE * raised_rows).reshape(TOKEN_SLOTS, ATTENTION_HEADS, HEAD_WIDTH)).astype(jnp.bfloat16)
        key_heads = rotary_embedded(projected_rows[:, 1].reshape(TOKEN_SLOTS, ATTENTION_HEADS, HEAD_WIDTH)).astype(jnp.bfloat16)
        value_heads = projected_rows[:, 2].reshape(TOKEN_SLOTS, ATTENTION_HEADS, HEAD_WIDTH).astype(jnp.bfloat16)
        scores = jnp.einsum('qhd,khd->hqk', query_head_rows.astype(jnp.float32), key_heads.astype(jnp.float32)) * HEAD_WIDTH ** (-0.5)
        allowed = (positions[None, :] <= positions[:, None]) & (positions[None, :] < length)
        scores = jnp.where(allowed[None], scores, MASKED)
        probabilities = jax.nn.softmax(scores, axis=-1).astype(jnp.bfloat16)
        attended = jnp.einsum('hqk,khd->qhd', probabilities.astype(jnp.float32), value_heads.astype(jnp.float32)).astype(jnp.bfloat16).reshape(TOKEN_SLOTS, D)
        head_parts = jnp.einsum('sgc,gcd->gsd', attended.reshape(TOKEN_SLOTS, N_MLP, group_heads).astype(jnp.float32), w_out.reshape(N_MLP, group_heads, D).astype(jnp.float32)).astype(jnp.bfloat16)
        head_parts = lax.optimization_barrier(head_parts)
        mixed_heads = lax.optimization_barrier(jnp.sum(head_parts.astype(jnp.float32), axis=0))
        stream = (residual_in + mixed_heads).astype(jnp.bfloat16)
        normed_mid = rms_norm(stream.astype(jnp.float32), norm_gain_mlp).astype(jnp.bfloat16)
        gate_up = jnp.dot(normed_mid, w_gateup.reshape(D, 2 * FF), preferred_element_type=jnp.float32).reshape(TOKEN_SLOTS, 2, FF)
        activated = (jax.nn.silu(gate_up[:, 0]) * gate_up[:, 1]).astype(jnp.bfloat16)
        unit_parts = jnp.einsum('sgc,gcd->gsd', activated.reshape(TOKEN_SLOTS, N_MLP, group_units).astype(jnp.float32), w_down.reshape(N_MLP, group_units, D).astype(jnp.float32)).astype(jnp.bfloat16)
        unit_parts = lax.optimization_barrier(unit_parts)
        unit_sum = lax.optimization_barrier(jnp.sum(unit_parts.astype(jnp.float32), axis=0))
        result = stream.astype(jnp.float32) + unit_sum
        out_slot = jnp.where((positions < length)[:, None], result, 0.0).astype(jnp.bfloat16)
        out_float = out_slot.astype(jnp.float32)
        slot_norm = jnp.sqrt(jnp.sum(out_float * out_float) / (length.astype(jnp.float32) * D))
        last_row = lax.dynamic_index_in_dim(out_float, (length - 1).astype(jnp.int32), 0, keepdims=False)
        last_normed = rms_norm(last_row, final_gain).astype(jnp.bfloat16)
        slot_peak = jnp.max(jnp.dot(vocab, last_normed, preferred_element_type=jnp.float32))
        return (out_slot, slot_norm, slot_peak)
    out_hidden, slot_norm, slot_peak = lax.map(one_slot, (hidden_in, slot_lengths, slot_tables))
    request_norm = jnp.zeros((R,), jnp.float32).at[slot_request].set(slot_norm)
    request_peak = jnp.zeros((R,), jnp.float32).at[slot_request].set(slot_peak)
    return (out_hidden, request_norm, request_peak)
```

```python
import functools
import math

import jax
import jax.numpy as jnp
import numpy as np
from jax import lax
from jax.experimental import pallas as pl
from jax.experimental.pallas import tpu as pltpu
from jax.sharding import PartitionSpec as P

HEAD_WIDTH = 64
EPSILON = 1e-05
ROPE_BASE = 130000.0
ADAPTER_SCALE = 2.0
MASKED = -1e30
F32, BF16 = jnp.float32, jnp.bfloat16
VMEM_LIMIT = 56 * 1024 * 1024

ME, Z, CORE, LENS = 0, 1, 2, 4
LAST_ROWS = 16


def nt(a, b):
    return lax.dot_general(a, b, (((1,), (1,)), ((), ())), preferred_element_type=F32)


def nn(a, b):
    return jnp.dot(a, b, preferred_element_type=F32)


def call(kernel, grid, ins, outs, shapes, scratch=(), flops=0, nbytes=0):
    spec = pltpu.PrefetchScalarGridSpec(
        num_scalar_prefetch=1, grid=grid, in_specs=ins, out_specs=outs, scratch_shapes=scratch
    )
    return pl.pallas_call(
        kernel,
        grid_spec=spec,
        out_shape=shapes,
        compiler_params=pltpu.CompilerParams(vmem_limit_bytes=VMEM_LIMIT),
        cost_estimate=pl.CostEstimate(
            flops=int(flops), bytes_accessed=int(nbytes), transcendentals=0
        ),
    )


def whole(shape):
    zeros = (0,) * len(shape)
    return pl.BlockSpec(tuple(shape), lambda *_: zeros)


def rope_tables(length):
    half = HEAD_WIDTH // 2
    frequency = np.float32(ROPE_BASE) ** (-(np.arange(half, dtype=np.float32) * 2.0 / HEAD_WIDTH))
    angles = np.arange(length, dtype=np.float32)[:, None] * frequency.astype(np.float32)[None, :]
    angles = angles.astype(np.float32)
    cosine, sine = np.cos(angles), np.sin(angles)
    return (
        np.concatenate([cosine] * 4, axis=1).astype(np.float32),
        np.concatenate([-sine, sine, -sine, sine], axis=1).astype(np.float32),
    )


def rotate(block, cosine, sine):
    lane = lax.broadcasted_iota(jnp.int32, block.shape, 1)
    front = (lane % HEAD_WIDTH) < HEAD_WIDTH // 2
    partner = jnp.where(
        front, pltpu.roll(block, 128 - HEAD_WIDTH // 2, 1), pltpu.roll(block, HEAD_WIDTH // 2, 1)
    )
    return block * cosine + partner * sine


def pick_kernel(slots, rows_at, table_rows, width, info, down, up, *outs):
    for j, out in enumerate(outs):
        for s in range(slots):
            slot = (info[ME] ^ j) * slots + s
            row = lax.rem(info[rows_at + slot], table_rows)
            out[s, :, :width] = down[row]
            out[s, :, width:] = up[row]


def project_kernel(
    info, x_ref, gain_ref, w_ref, cos_ref, sin_ref, k_ref, v_ref, q_ref, normed_ref, held
):
    part, i = pl.program_id(0), pl.program_id(1)
    rows = x_ref.shape[0]
    at = pl.ds(pl.multiple_of(i * rows, rows), rows)

    @pl.when(part == 0)
    def _():
        x = x_ref[...].astype(F32)
        mean = jnp.mean(x * x, axis=-1, keepdims=True)
        normed = (x * lax.rsqrt(mean + EPSILON) * gain_ref[...]).astype(BF16)
        held[at] = normed
        normed_ref[...] = normed

    product = nn(held[at], w_ref[0])

    @pl.when(part == 0)
    def _():
        for g in range(product.shape[1] // 128):
            lanes = slice(g * 128, g * 128 + 128)
            k_ref[:, lanes] = rotate(product[:, lanes], cos_ref[...], sin_ref[...]).astype(BF16)

    @pl.when(part == 1)
    def _():
        v_ref[...] = product.astype(BF16)

    @pl.when(part == 2)
    def _():
        q_ref[...] = product


def attend_kernel(
    slots, rows_at, table_rows, n, info, q_ref, k_ref, v_ref, normed_ref, cos_ref, sin_ref, *rest
):
    received, (out_ref, queries, factors) = rest[:n], rest[n:]
    s = pl.program_id(0)
    length, columns = q_ref.shape
    width = normed_ref.shape[1]
    table_row = info[rows_at + info[ME] * slots + s]
    source = info[ME] ^ lax.div(table_row, table_rows)
    for j in range(n):

        @pl.when(source == j)
        def _(j=j):
            factors[...] = received[j][s]

    low_rank = nt(normed_ref[...], factors[:, :width]).astype(BF16)
    raised = nn(low_rank, factors[:, width:])
    full = q_ref[...] + ADAPTER_SCALE * raised
    for g in range(columns // 128):
        lanes = slice(g * 128, g * 128 + 128)
        queries[:, lanes] = rotate(full[:, lanes], cos_ref[...], sin_ref[...]).astype(BF16)
    step = 128
    scale = HEAD_WIDTH ** (-0.5) * math.log2(math.e)

    def pair(g, carry):
        lanes = pl.ds(pl.multiple_of(g * 128, 128), 128)
        for b in range(length // step):
            keys = (b + 1) * step
            q = queries[b * step : keys, lanes]
            first = lax.broadcasted_iota(jnp.int32, q.shape, 1) < HEAD_WIDTH
            zero = jnp.zeros_like(q)
            both = jnp.concatenate([jnp.where(first, q, zero), jnp.where(first, zero, q)], axis=0)
            scores = nt(both, k_ref[0:keys, lanes]) * scale
            row = lax.broadcasted_iota(jnp.int32, scores.shape, 0) % step + b * step
            col = lax.broadcasted_iota(jnp.int32, scores.shape, 1)
            scores = jnp.where(col <= row, scores, MASKED)
            top = jnp.max(scores, axis=1, keepdims=True)
            weights = jnp.exp2(scores - top)
            total = jnp.sum(weights, axis=1, keepdims=True)
            mixed = nn(weights.astype(BF16), v_ref[0:keys, lanes]) / total
            out_ref[b * step : keys, lanes] = jnp.where(first, mixed[:step], mixed[step:]).astype(
                BF16
            )
        return carry

    lax.fori_loop(0, columns // 128, pair, 0)


def targets(info, row, slots, length, core):
    place = jnp.full(row.shape, -1, jnp.int32)
    for s in range(slots):
        g = core * slots + s
        live = info[LENS + g]
        off = info[LENS + 2 * slots + g]
        inside = (row >= off) & (row < off + live)
        place = jnp.where(inside, row - off + s * length, place)
        place = jnp.where(row == g, s * length + live - 1, place)
    return place


def one_hot(place, columns):
    col = lax.broadcasted_iota(jnp.int32, (place.shape[0], columns), 1)
    return jnp.where(col == place, 1.0, 0.0).astype(BF16)


def hidden_kernel(slots, nz, starts, sizes, info, hidden_ref, *outs):
    count = len(sizes)
    length = hidden_ref.shape[0] // slots
    core = info[CORE]
    for k in range(count):
        quarter = sizes[k] // nz
        for whose in range(2):
            target_core = core if whose == 0 else 1 - core
            base = starts[k] * 2 + target_core * sizes[k] + info[Z] * quarter
            row = lax.broadcasted_iota(jnp.int32, (quarter, 1), 0) + base
            place = targets(info, row, slots, length, core)
            outs[whose * count + k][...] = nn(
                one_hot(place, hidden_ref.shape[0]), hidden_ref[...]
            ).astype(BF16)


def mix_kernel(slots, start, size, info, own_ref, other_ref, w_ref, out_ref):
    length = own_ref.shape[0] // slots
    core = info[CORE]
    row = lax.broadcasted_iota(jnp.int32, (size, 1), 0) + start * 2 + core * size
    packed = nn(
        one_hot(targets(info, row, slots, length, core), own_ref.shape[0]), own_ref[...]
    ) + nn(
        one_hot(targets(info, row, slots, length, 1 - core), own_ref.shape[0]), other_ref[...]
    )
    product = nn(packed.astype(BF16), w_ref[...]).astype(BF16)
    out_ref[...] = product.reshape(out_ref.shape)


def stream_kernel(info, part_ref, right, left, own, other, gain, stream_ref, normed_ref):
    mixed = part_ref[0].astype(F32) + right[...].astype(F32) + left[...].astype(F32)
    hidden = own[...].astype(F32) + other[...].astype(F32)
    stream = (hidden + mixed).astype(BF16)
    stream_ref[...] = stream
    x = stream.astype(F32)
    mean = jnp.mean(x * x, axis=-1, keepdims=True)
    normed_ref[...] = (x * lax.rsqrt(mean + EPSILON) * gain[...]).astype(BF16)


def finish_kernel(slots, start, size, info, part_ref, right, left, stream, out_ref, sums_ref):
    quarter, width = stream.shape
    total = part_ref[0].astype(F32) + right[...].astype(F32) + left[...].astype(F32)
    result = stream[...].astype(F32) + total
    row = lax.broadcasted_iota(jnp.int32, (quarter, 1), 0)
    row = row + start * 2 + info[CORE] * size + info[Z] * quarter
    keep = row < 2 * slots
    belongs = []
    for g in range(2 * slots):
        live, off = info[LENS + g], info[LENS + 2 * slots + g]
        inside = (row >= off) & (row < off + live)
        belongs.append(inside)
        keep = keep | inside
    rounded = jnp.where(keep, result, 0.0).astype(BF16)
    out_ref[...] = rounded
    wide = rounded.astype(F32)
    squares = jnp.sum(wide * wide, axis=1, keepdims=True)
    lane = lax.broadcasted_iota(jnp.int32, sums_ref.shape, 1)
    sums = jnp.zeros(sums_ref.shape, F32)
    for g in range(2 * slots):
        sums = jnp.where(lane == g, jnp.sum(jnp.where(belongs[g], squares, 0.0)), sums)
    sums_ref[...] = sums


def unit_kernel(nz, info, own, *rest):
    rights, lefts = rest[: nz - 1], rest[nz - 1 : 2 * nz - 2]
    w_ref, out_ref, x, acc = rest[2 * nz - 2 :]
    b = pl.program_id(0)
    quarter = own.shape[0]
    z = info[Z]

    @pl.when(b == 0)
    def _():
        for place in range(nz):
            at = slice(place * quarter, (place + 1) * quarter)

            @pl.when(z == place)
            def _(at=at):
                x[at] = own[...]

            for d in range(1, nz):

                @pl.when(z - place == d)
                def _(at=at, d=d):
                    x[at] = rights[d - 1][...]

                @pl.when(place - z == d)
                def _(at=at, d=d):
                    x[at] = lefts[d - 1][...]

    depth = w_ref.shape[1] // 3
    columns = w_ref.shape[2]
    width = x.shape[1]
    gate = nn(x[...], w_ref[:, 0:depth].reshape(width, columns))
    up = nn(x[...], w_ref[:, depth : 2 * depth].reshape(width, columns))
    active = (gate / (1.0 + jnp.exp(-gate)) * up).astype(BF16)
    product = nt(active, w_ref[:, 2 * depth :].reshape(width, columns))

    @pl.when(b == 0)
    def _():
        acc[...] = product

    @pl.when(b > 0)
    def _():
        acc[...] += product

    @pl.when(b == pl.num_programs(0) - 1)
    def _():
        out_ref[...] = acc[...].astype(BF16).reshape(out_ref.shape)


def take(parts, index):
    return lax.dynamic_index_in_dim(parts, index, 0, keepdims=False)


def reduce_to_owners(parts, z, nz):
    right = left = None
    for s in range(1, nz):
        message = take(parts, jnp.clip(nz - s + z, 0, nz - 1))
        right = lax.ppermute(
            message if right is None else message + right, "mlp", [(i, i + 1) for i in range(s)]
        )
        message = take(parts, jnp.clip(s + z - nz, 0, nz - 1))
        left = lax.ppermute(
            message if left is None else message + left,
            "mlp",
            [(nz - 1 - i, nz - 2 - i) for i in range(s)],
        )
    return right, left


def spread(own, nz):
    rights, lefts = [own], [own]
    for s in range(1, nz):
        rights.append(lax.ppermute(rights[-1], "mlp", [(i, i + 1) for i in range(s - 1, nz - 1)]))
        lefts.append(lax.ppermute(lefts[-1], "mlp", [(i + 1, i) for i in range(0, nz - s)]))
    return rights[1:], lefts[1:]


def body(total, info, hidden, slot_request, gains, w_qkv, w_out, merged, tables, vocab, sizes_n):
    n, nz = sizes_n
    gain_attn, gain_mlp, final_gain = gains
    down, up = tables
    slots, length, width = hidden.shape
    rows = slots * length
    columns = w_qkv.shape[2]
    rank = down.shape[1]
    table_rows = down.shape[0]
    rows_at = LENS + 4 * slots
    me, z = lax.axis_index("req"), lax.axis_index("mlp")
    core = me % 2
    swap = [(i, i ^ 1) for i in range(n)]
    half = -(-total // 128) * 64
    sizes = [half, total - half]
    starts = [0, half]
    count = len(sizes)

    weights = lax.all_gather(merged, "req", axis=0)

    factor_shape = (slots, rank, width + columns)
    picked = call(
        functools.partial(pick_kernel, slots, rows_at, table_rows, width),
        (1,),
        [whole(down.shape), whole(up.shape)],
        [whole(factor_shape)] * n,
        [jax.ShapeDtypeStruct(factor_shape, BF16)] * n,
    )(info, down, up)
    received = [picked[0]] + [
        lax.ppermute(picked[j], "req", [(i, i ^ j) for i in range(n)]) for j in range(1, n)
    ]

    cosine, sine = rope_tables(length)
    block = 256
    blocks = rows // block
    per_slot = length // block
    last = blocks - 1
    keys, values, queries, normed = call(
        project_kernel,
        (3, blocks),
        [
            pl.BlockSpec((block, width), lambda p, i, _: (jnp.where(p == 0, i, last), 0)),
            whole((1, width)),
            pl.BlockSpec((1, width, columns), lambda p, i, _: ((p + 1) % 3, 0, 0)),
            pl.BlockSpec((block, 128), lambda p, i, _: (i % per_slot, 0)),
            pl.BlockSpec((block, 128), lambda p, i, _: (i % per_slot, 0)),
        ],
        [
            pl.BlockSpec((block, columns), lambda p, i, _: (jnp.where(p == 0, i, last), 0)),
            pl.BlockSpec(
                (block, columns),
                lambda p, i, _: (jnp.where(p == 0, 0, jnp.where(p == 1, i, last)), 0),
            ),
            pl.BlockSpec((block, columns), lambda p, i, _: (jnp.where(p == 2, i, 0), 0)),
            pl.BlockSpec((block, width), lambda p, i, _: (jnp.where(p == 0, i, last), 0)),
        ],
        [
            jax.ShapeDtypeStruct((rows, columns), BF16),
            jax.ShapeDtypeStruct((rows, columns), BF16),
            jax.ShapeDtypeStruct((rows, columns), F32),
            jax.ShapeDtypeStruct((rows, width), BF16),
        ],
        [pltpu.VMEM((rows, width), BF16)],
        flops=2 * rows * width * 3 * columns,
        nbytes=2 * (2 * rows * width + 3 * width * columns),
    )(info, hidden.reshape(rows, width), gain_attn, w_qkv, cosine, sine)

    by_slot = lambda w: pl.BlockSpec((length, w), lambda s, _: (s, 0))
    attended = call(
        functools.partial(attend_kernel, slots, rows_at, table_rows, n),
        (slots,),
        [by_slot(columns)] * 3
        + [by_slot(width), whole((length, 128)), whole((length, 128))]
        + [whole(factor_shape)] * n,
        by_slot(columns),
        jax.ShapeDtypeStruct((rows, columns), BF16),
        [pltpu.VMEM((length, columns), BF16), pltpu.VMEM(factor_shape[1:], BF16)],
        flops=8 * rows * length * columns,
        nbytes=2 * rows * (width + 5 * columns),
    )(info, queries, keys, values, normed, cosine, sine, *received)
    other = lax.ppermute(attended, "req", swap)

    quarters = [size // nz for size in sizes]
    quarter_shapes = [jax.ShapeDtypeStruct((q, width), BF16) for q in quarters]
    quarter_specs = [whole((q, width)) for q in quarters]
    shared = call(
        functools.partial(hidden_kernel, slots, nz, starts, sizes),
        (1,),
        [whole((rows, width))],
        quarter_specs * 2,
        quarter_shapes * 2,
        flops=4 * sum(quarters) * rows * width,
        nbytes=2 * rows * width,
    )(info, hidden.reshape(rows, width))
    hidden_own = shared[:count]
    hidden_other = [lax.ppermute(piece, "req", swap) for piece in shared[count:]]

    def own_part(q):
        return pl.BlockSpec((1, q, width), lambda i, info: (info[Z], 0, 0))

    outs, sums = [], 0.0
    for k in range(count):
        q, size, spec = quarters[k], sizes[k], quarter_specs[k]
        part_shape = jax.ShapeDtypeStruct((nz, q, width), BF16)
        head_parts = call(
            functools.partial(mix_kernel, slots, starts[k], size),
            (1,),
            [whole((rows, columns))] * 2 + [whole(w_out.shape)],
            whole(part_shape.shape),
            part_shape,
            flops=2 * size * columns * (2 * rows + width),
            nbytes=2 * (columns * (2 * rows + width) + size * width),
        )(info, attended, other, w_out)
        right, left = reduce_to_owners(head_parts, z, nz)
        stream, mid = call(
            stream_kernel,
            (1,),
            [own_part(q)] + [spec] * 4 + [whole((1, width))],
            [spec, spec],
            [quarter_shapes[k]] * 2,
            nbytes=14 * q * width,
        )(info, head_parts, right, left, hidden_own[k], hidden_other[k], gain_mlp)
        rights, lefts = spread(mid, nz)
        unit = 256
        unit_parts = call(
            functools.partial(unit_kernel, nz),
            (weights.shape[2] // unit,),
            [spec] * (2 * nz - 1)
            + [pl.BlockSpec(weights.shape[:2] + (unit,), lambda b, _: (0, 0, b))],
            whole(part_shape.shape),
            part_shape,
            [pltpu.VMEM((size, width), BF16), pltpu.VMEM((size, width), F32)],
            flops=6 * size * width * weights.shape[2],
            nbytes=2 * weights.size,
        )(info, mid, *rights, *lefts, weights)
        right, left = reduce_to_owners(unit_parts, z, nz)
        out, sum_k = call(
            functools.partial(finish_kernel, slots, starts[k], size),
            (1,),
            [own_part(q)] + [spec] * 3,
            [spec, whole((8, 128))],
            [quarter_shapes[k], jax.ShapeDtypeStruct((8, 128), F32)],
            nbytes=10 * q * width,
        )(info, unit_parts, right, left, stream)
        sums = sums + sum_k
        rights, lefts = spread(out, nz)
        line = jnp.concatenate(rights[::-1] + [out] + lefts, axis=0)
        mine = lax.dynamic_slice_in_dim(line, (nz - 1 - z) * q, nz * q, 0)
        theirs = lax.ppermute(mine, "req", swap)
        outs.append(jnp.where(core == 0, mine, theirs))
        outs.append(jnp.where(core == 0, theirs, mine))

    slots_all = slot_request.shape[0]
    chip_rows = outs[0][: 2 * slots].astype(F32)
    chip_last = (
        chip_rows
        * lax.rsqrt(jnp.mean(chip_rows * chip_rows, axis=-1, keepdims=True) + EPSILON)
        * final_gain
    ).astype(BF16)
    every = jnp.zeros((slots_all, width), BF16)
    every = lax.dynamic_update_slice_in_dim(every, chip_last, (me // 2) * 2 * slots, 0)
    bit = 2
    while bit < n:
        every = every + lax.ppermute(every, "req", [(i, i ^ bit) for i in range(n)])
        bit *= 2
    peaks = jnp.max(nt(every, vocab), axis=1)
    norm_sums = jnp.zeros((slots_all,), F32)
    norm_sums = lax.dynamic_update_slice_in_dim(
        norm_sums, sums[0, : 2 * slots], (me // 2) * 2 * slots, 0
    )
    bit = 1
    while bit < n * nz:
        if bit < n:
            axis, pairs = "req", [(i, i ^ bit) for i in range(n)]
        else:
            axis, pairs = "mlp", [(i, i ^ (bit // n)) for i in range(nz)]
        arrived = lax.ppermute(jnp.stack([norm_sums, peaks]), axis, pairs)
        norm_sums = norm_sums + arrived[0]
        peaks = jnp.maximum(peaks, arrived[1])
        bit *= 2

    packed = jnp.concatenate(outs + [jnp.zeros((length, width), BF16)], axis=0)
    result = []
    for s in range(slots):
        g = core * slots + s
        piece = lax.dynamic_slice_in_dim(packed, info[LENS + 2 * slots + g], length, 0)
        live = jnp.arange(length, dtype=jnp.int32) < info[LENS + g]
        result.append(jnp.where(live[:, None], piece, jnp.zeros((), BF16)))
    return jnp.stack(result), norm_sums, peaks


def per_device(sizes_n, *arrays):
    (hidden, lengths, slot_request, adapter_of, adapter_slot, gain_attn, gain_mlp, final_gain) = (
        arrays[:8]
    )
    (w_qkv, w_out, w_gateup, w_down, adapter_down, adapter_up, vocab) = arrays[8:]
    slots, length, width = hidden.shape
    me, z = lax.axis_index("req"), lax.axis_index("mlp")

    def look_up(table, index):
        at = jnp.arange(table.shape[0], dtype=jnp.int32)
        return jnp.sum(jnp.where(index[:, None] == at[None, :], table[None, :], 0), axis=1)

    slot_lengths = look_up(lengths, slot_request)
    table_rows = look_up(adapter_slot, look_up(adapter_of, slot_request))
    aligned = ((slot_lengths + 15) // 16 * 16).reshape(-1, 2 * slots)
    before = jnp.arange(2 * slots)[:, None] < jnp.arange(2 * slots)[None, :]
    offsets = LAST_ROWS + jnp.sum(
        jnp.where(before[None], aligned[:, :, None], 0), axis=1, dtype=jnp.int32
    )
    needed = jnp.max(LAST_ROWS + jnp.sum(aligned, axis=1))
    chip = jnp.arange(aligned.shape[0]) == me // 2
    own = lambda values: jnp.sum(
        jnp.where(chip[:, None], values.reshape(-1, 2 * slots), 0), axis=0, dtype=jnp.int32
    )
    info = jnp.concatenate(
        [
            jnp.stack([me, z, me % 2, needed]).astype(jnp.int32),
            own(slot_lengths),
            own(offsets),
            table_rows,
        ]
    )
    merged = jnp.concatenate([w_gateup[:, 0], w_gateup[:, 1], w_down.T], axis=0)
    largest = -(-(2 * slots * length + LAST_ROWS) // 128) * 64
    out, norm_sums, peaks = body(
        largest,
        info,
        hidden,
        slot_request,
        tuple(g.reshape(1, width) for g in (gain_attn, gain_mlp, final_gain)),
        w_qkv.transpose(1, 0, 2),
        w_out,
        merged,
        (adapter_down, adapter_up),
        vocab,
        sizes_n,
    )
    slot_norm = jnp.sqrt(norm_sums / (slot_lengths.astype(F32) * width))
    requests = jnp.arange(slot_request.shape[0], dtype=jnp.int32)
    owners = slot_request[None, :] == requests[:, None]
    request_norm = jnp.sum(jnp.where(owners, slot_norm[None, :], 0.0), axis=1)
    request_peak = jnp.sum(jnp.where(owners, peaks[None, :], 0.0), axis=1)
    return out, request_norm, request_peak


def solution(mesh):
    return jax.shard_map(
        functools.partial(per_device, (mesh.shape["req"], mesh.shape["mlp"])),
        mesh=mesh,
        in_specs=(
            P("req", None, None),
            P(),
            P(),
            P(),
            P(),
            P(),
            P(),
            P(),
            P(None, None, "mlp"),
            P("mlp", None),
            P("req", None, "mlp"),
            P("mlp", "req"),
            P("req", None, None),
            P("req", None, "mlp"),
            P(("req", "mlp"), None),
        ),
        out_specs=(P("req", None, None), P(), P()),
        check_vma=False,
    )
```

```python
import functools
import math

import jax
import jax.numpy as jnp
import numpy as np
from jax import lax
from jax.experimental import pallas as pl
from jax.experimental.pallas import tpu as pltpu
from jax.sharding import PartitionSpec as P

HEAD_WIDTH = 64
EPSILON = 1e-05
ROPE_BASE = 130000.0
ADAPTER_SCALE = 2.0
MASKED = -1e30
F32, BF16 = jnp.float32, jnp.bfloat16
UNIT = 256
CLASSES = [(7, 5, 0), (8, 5, 0), (8, 6, 0), (8, 8, 64)]
VMEM_LIMIT = 36 * 1024 * 1024

ME, Z, CORE, CLASS, TABLES = 0, 1, 2, 3, 8
LAST_ROWS = 16
ANY = pl.BlockSpec(memory_space=pl.ANY)
SMEM = pl.BlockSpec(memory_space=pltpu.SMEM)


def nt(a, b):
    return lax.dot_general(a, b, (((1,), (1,)), ((), ())), preferred_element_type=F32)


def nn(a, b):
    return jnp.dot(a, b, preferred_element_type=F32)


def call(kernel, grid, ins, outs, shapes, scratch=(), flops=0, nbytes=0, aliases=None):
    spec = pltpu.PrefetchScalarGridSpec(
        num_scalar_prefetch=1, grid=grid, in_specs=ins, out_specs=outs, scratch_shapes=scratch
    )
    return pl.pallas_call(
        kernel,
        grid_spec=spec,
        out_shape=shapes,
        input_output_aliases=aliases or {},
        compiler_params=pltpu.CompilerParams(vmem_limit_bytes=VMEM_LIMIT),
        cost_estimate=pl.CostEstimate(
            flops=int(flops), bytes_accessed=int(nbytes), transcendentals=0
        ),
    )


def whole(shape):
    zeros = (0,) * len(shape)
    return pl.BlockSpec(tuple(shape), lambda *_: zeros)


def rope_tables(length):
    half = HEAD_WIDTH // 2
    frequency = np.float32(ROPE_BASE) ** (-(np.arange(half, dtype=np.float32) * 2.0 / HEAD_WIDTH))
    angles = np.arange(length, dtype=np.float32)[:, None] * frequency.astype(np.float32)[None, :]
    angles = angles.astype(np.float32)
    cosine, sine = np.cos(angles), np.sin(angles)
    return (
        np.concatenate([cosine] * 4, axis=1).astype(np.float32),
        np.concatenate([-sine, sine, -sine, sine], axis=1).astype(np.float32),
    )


def rotate(block, cosine, sine):
    lane = lax.broadcasted_iota(jnp.int32, block.shape, 1)
    front = (lane % HEAD_WIDTH) < HEAD_WIDTH // 2
    partner = jnp.where(
        front, pltpu.roll(block, 128 - HEAD_WIDTH // 2, 1), pltpu.roll(block, HEAD_WIDTH // 2, 1)
    )
    return block * cosine + partner * sine


def live_at(slots, h, g):
    return TABLES + slots + h * 4 * slots + g


def place_at(slots, h, g):
    return TABLES + slots + h * 4 * slots + 2 * slots + g


def setup_kernel(
    slots, half, classes, me_ref, z_ref, lengths, slot_request, adapter_of, adapter_slot, down, up,
    info, *outs
):
    table_rows, _, width = down.shape
    me, z = me_ref[0], z_ref[0]
    core, chip = lax.rem(me, 2), lax.div(me, 2)
    chip_slots = 2 * slots
    info[ME], info[Z], info[CORE] = me, z, core

    def split(slot):
        live = lengths[slot_request[slot]]
        first = jnp.minimum(live, half)
        return first, live - first

    def aligned(live):
        return lax.div(live + 15, 16) * 16

    most = [jnp.int32(0), jnp.int32(0)]
    for c in range(slot_request.shape[0] // chip_slots):
        total = [jnp.int32(0), jnp.int32(LAST_ROWS)]
        for g in range(chip_slots):
            for h, live in enumerate(split(c * chip_slots + g)):
                total[h] = total[h] + aligned(live)
        most = [jnp.maximum(most[h], total[h]) for h in range(2)]
    choice = jnp.int32(len(classes) - 1)
    for i in reversed(range(len(classes) - 1)):
        fits = (most[0] <= 2 * classes[i][0]) & (most[1] <= 2 * classes[i][1])
        choice = jnp.where(fits, i, choice)
    info[CLASS] = choice
    total = [jnp.int32(0), jnp.int32(LAST_ROWS)]
    for g in range(chip_slots):
        for h, live in enumerate(split(chip * chip_slots + g)):
            info[live_at(slots, h, g)] = live
            info[place_at(slots, h, g)] = total[h]
            total[h] = total[h] + aligned(live)
    for s in range(slots):
        info[TABLES + s] = adapter_slot[adapter_of[slot_request[me * slots + s]]]
    for j, out in enumerate(outs):
        for s in range(slots):
            slot = (me ^ j) * slots + s
            row = lax.rem(adapter_slot[adapter_of[slot_request[slot]]], table_rows)
            out[s, :, :width] = down[row]
            out[s, :, width:] = up[row]


def merge_kernel(info, gate_up, down, after, out):
    depth, units = down.shape[1], down.shape[0]
    for b in range(units // UNIT):
        at = slice(b * UNIT, (b + 1) * UNIT)
        out[b, 0:depth] = gate_up[:, 0, at]
        out[b, depth : 2 * depth] = gate_up[:, 1, at]
        out[b, 2 * depth :] = down[at, :] if depth == UNIT else down[at, :].T


def project_kernel(
    info, x_ref, gain_ref, w_ref, cos_ref, sin_ref, k_ref, v_ref, q_ref, normed_ref
):
    slots, rows, width = x_ref.shape
    group = 64
    for s in range(slots):
        for i in range(rows // group):
            x = x_ref[s, i * group : (i + 1) * group].astype(F32)
            mean = jnp.mean(x * x, axis=-1, keepdims=True)
            at = slice(s * rows + i * group, s * rows + (i + 1) * group)
            normed_ref[at] = (x * lax.rsqrt(mean + EPSILON) * gain_ref[...]).astype(BF16)
    product = nn(normed_ref[...], w_ref[1])
    for s in range(slots):
        at = slice(s * rows, (s + 1) * rows)
        for g in range(product.shape[1] // 128):
            lanes = slice(g * 128, g * 128 + 128)
            k_ref[at, lanes] = rotate(product[at, lanes], cos_ref[...], sin_ref[...]).astype(BF16)
    v_ref[...] = nn(normed_ref[...], w_ref[2]).astype(BF16)
    q_ref[...] = nn(normed_ref[...], w_ref[0])


def attend_kernel(slots, table_rows, n, h, info, after_one, after_two, q_ref, normed_ref, cos_ref, sin_ref, *rest):
    keys, values, received = rest[: h + 1], rest[h + 1 : 2 * h + 2], rest[2 * h + 2 : 2 * h + 2 + n]
    out_ref, queries, factors = rest[-3:]
    s = pl.program_id(0)
    length, columns = q_ref.shape
    width = normed_ref.shape[1]
    source = info[ME] ^ lax.div(info[TABLES + s], table_rows)
    for j in range(n):

        @pl.when(source == j)
        def _(j=j):
            factors[...] = received[j][s]

    low_rank = nt(normed_ref[...], factors[:, :width]).astype(BF16)
    raised = nn(low_rank, factors[:, width:])
    full = q_ref[...] + ADAPTER_SCALE * raised
    for g in range(columns // 128):
        lanes = slice(g * 128, g * 128 + 128)
        queries[:, lanes] = rotate(full[:, lanes], cos_ref[...], sin_ref[...]).astype(BF16)
    step = length
    scale = HEAD_WIDTH ** (-0.5) * math.log2(math.e)

    def pair(g):
        lanes = slice(g * 128, g * 128 + 128)
        for b in range(length // step):
            end = (b + 1) * step
            q = queries[b * step : end, lanes]
            first = lax.broadcasted_iota(jnp.int32, q.shape, 1) < HEAD_WIDTH
            zero = jnp.zeros_like(q)
            both = jnp.concatenate([jnp.where(first, q, zero), jnp.where(first, zero, q)], axis=0)
            scores = nt(both, keys[h][0:end, lanes]) * scale
            row = lax.broadcasted_iota(jnp.int32, scores.shape, 0) % step + b * step
            col = lax.broadcasted_iota(jnp.int32, scores.shape, 1)
            scores = [jnp.where(col <= row, scores, MASKED)]
            used = [values[h][0:end, lanes]]
            for before in range(h):
                scores.append(nt(both, keys[before][:, lanes]) * scale)
                used.append(values[before][:, lanes])
            top = functools.reduce(
                jnp.maximum, [jnp.max(part, axis=1, keepdims=True) for part in scores]
            )
            weights = [jnp.exp2(part - top) for part in scores]
            total = sum(jnp.sum(part, axis=1, keepdims=True) for part in weights)
            mixed = sum(nn(part.astype(BF16), value) for part, value in zip(weights, used))
            mixed = mixed / total
            out_ref[b * step : end, lanes] = jnp.where(first, mixed[:step], mixed[step:]).astype(
                BF16
            )

    for g in range(columns // 128):
        pair(g)


def targets(info, row, slots, h, half, core, stride, start):
    place = jnp.full(row.shape, -1, jnp.int32)
    for s in range(slots):
        g = core * slots + s
        live = info[live_at(slots, h, g)]
        at = info[place_at(slots, h, g)]
        inside = (row >= at) & (row < at + live)
        place = jnp.where(inside, row - at + s * stride + start, place)
    return place


def last_targets(info, row, slots, half, core, h, stride, start):
    place = jnp.full(row.shape, -1, jnp.int32)
    for s in range(slots):
        g = core * slots + s
        second = info[live_at(slots, 1, g)]
        live = info[live_at(slots, 0, g)] if h == 0 else second
        there = (second > 0) if h == 1 else (second == 0)
        place = jnp.where((row == g) & there, s * stride + start + live - 1, place)
    return place


def one_hot(place, columns):
    col = lax.broadcasted_iota(jnp.int32, (place.shape[0], columns), 1)
    return jnp.where(col == place, 1.0, 0.0).astype(BF16)


def hidden_kernel(slots, nz, sizes, info, hidden_ref, *outs):
    count = len(sizes)
    tokens = hidden_ref.shape[0]
    length = tokens // slots
    half = length // 2
    core = info[CORE]
    for h in range(count):
        quarter = sizes[h] // nz
        for whose in range(2):
            target_core = core if whose == 0 else 1 - core
            base = target_core * sizes[h] + info[Z] * quarter
            row = lax.broadcasted_iota(jnp.int32, (quarter, 1), 0) + base
            place = targets(info, row, slots, h, half, core, length, h * half)
            if h == 1:
                for part in range(2):
                    late = last_targets(info, row, slots, half, core, part, length, part * half)
                    place = jnp.maximum(place, late)
            outs[whose * count + h][...] = nn(one_hot(place, tokens), hidden_ref[...]).astype(BF16)


def mix_kernel(slots, size, h, info, after, w_ref, *rest):
    parts, out_ref = rest[:-1], rest[-1]
    tokens = parts[0].shape[0]
    half = tokens // slots
    core = info[CORE]
    cores = (core, 1 - core)
    row = lax.broadcasted_iota(jnp.int32, (size, 1), 0) + core * size
    packed = 0.0
    for whose in range(2):
        place = targets(info, row, slots, h, half, cores[whose], half, 0)
        if h == 1:
            late = last_targets(info, row, slots, half, cores[whose], 1, half, 0)
            place = jnp.maximum(place, late)
        packed = packed + nn(one_hot(place, tokens), parts[whose][...])
    if h == 1:
        front = 0.0
        for whose in range(2):
            place = last_targets(info, row[:LAST_ROWS], slots, half, cores[whose], 0, half, 0)
            front = front + nn(one_hot(place, tokens), parts[2 + whose][...])
        packed = jnp.concatenate([packed[:LAST_ROWS] + front, packed[LAST_ROWS:]], axis=0)
    product = nn(packed.astype(BF16), w_ref[...]).astype(BF16)
    out_ref[...] = product.reshape(out_ref.shape)


def stream_kernel(info, part_ref, right, left, own, other, gain, stream_ref, normed_ref):
    mixed = part_ref[0].astype(F32) + right[...].astype(F32) + left[...].astype(F32)
    hidden = own[...].astype(F32) + other[...].astype(F32)
    stream = (hidden + mixed).astype(BF16)
    stream_ref[...] = stream
    x = stream.astype(F32)
    mean = jnp.mean(x * x, axis=-1, keepdims=True)
    normed_ref[...] = (x * lax.rsqrt(mean + EPSILON) * gain[...]).astype(BF16)


def finish_kernel(slots, size, h, info, part_ref, right, left, stream, gain, out_ref, sums_ref, *lasts):
    quarter, width = stream.shape
    chip_slots = 2 * slots
    total = part_ref[0].astype(F32) + right[...].astype(F32) + left[...].astype(F32)
    result = stream[...].astype(F32) + total
    base = info[CORE] * size + info[Z] * quarter
    row = lax.broadcasted_iota(jnp.int32, (quarter, 1), 0) + base
    keep = (row < chip_slots) if h == 1 else (row < 0)
    belongs = []
    for g in range(chip_slots):
        live, at = info[live_at(slots, h, g)], info[place_at(slots, h, g)]
        inside = (row >= at) & (row < at + live)
        belongs.append(inside)
        keep = keep | inside
    rounded = jnp.where(keep, result, 0.0).astype(BF16)
    out_ref[...] = rounded
    wide = rounded.astype(F32)
    squares = jnp.sum(wide * wide, axis=1, keepdims=True)
    lane = lax.broadcasted_iota(jnp.int32, sums_ref.shape, 1)
    first_slot = lax.div(info[ME], 2) * chip_slots
    sums = jnp.zeros(sums_ref.shape, F32)
    for g in range(chip_slots):
        part = jnp.sum(jnp.where(belongs[g], squares, 0.0))
        sums = jnp.where(lane == first_slot + g, part, sums)
    sums_ref[...] = sums
    for last_ref in lasts:
        last_ref[...] = jnp.zeros(last_ref.shape, BF16)
        front = wide[:LAST_ROWS]
        mean = jnp.mean(front * front, axis=-1, keepdims=True)
        last = (front * lax.rsqrt(mean + EPSILON) * gain[...]).astype(BF16)
        slot = lax.broadcasted_iota(jnp.int32, (last_ref.shape[0], LAST_ROWS), 0) - first_slot
        kept = lax.broadcasted_iota(jnp.int32, slot.shape, 1)
        pick = jnp.where((slot == kept) & (kept < chip_slots), 1.0, 0.0).astype(BF16)

        @pl.when(base == 0)
        def _():
            last_ref[...] = nn(pick, last).astype(BF16)


def in_order(nz, z, own, rights, lefts, out, sems):
    quarter = own.shape[0]

    def copy(piece, place):
        return pltpu.make_async_copy(
            piece, out.at[pl.ds(place * quarter, quarter)], sems.at[place]
        )

    for place in range(nz):

        @pl.when(z == place)
        def _(place=place):
            copy(own, place).start()

        for d in range(1, nz):

            @pl.when(z - place == d)
            def _(place=place, d=d):
                copy(rights[d - 1], place).start()

            @pl.when(place - z == d)
            def _(place=place, d=d):
                copy(lefts[d - 1], place).start()

    for place in range(nz):
        copy(own, place).wait()


def order_kernel(nz, info, own, *rest):
    rights, lefts, (out, sems) = rest[: nz - 1], rest[nz - 1 : 2 * nz - 2], rest[2 * nz - 2 :]
    in_order(nz, info[Z], own, rights, lefts, out, sems)


def unpack_kernel(slots, h, info, mine, theirs, *rest):
    out, packed, sems = rest[-3:]
    s = pl.program_id(0)
    size = mine.shape[0]
    core = info[CORE]

    @pl.when(s == 0)
    def _():
        copies = [
            pltpu.make_async_copy(
                piece,
                packed.at[pl.ds(pl.multiple_of(place * size, 16), size)],
                sems.at[i],
            )
            for i, (piece, place) in enumerate(((mine, core), (theirs, 1 - core)))
        ]
        for copy in copies:
            copy.start()
        for copy in copies:
            copy.wait()

    g = core * slots + s
    live, at = info[live_at(slots, h, g)], info[place_at(slots, h, g)]
    rows = packed[pl.ds(pl.multiple_of(at, 16), out.shape[0])]
    row = lax.broadcasted_iota(jnp.int32, (out.shape[0], 1), 0)
    out[...] = jnp.where(row < live, rows, jnp.zeros((), BF16))


def unit_kernel(nz, info, own, *rest):
    rights, lefts = rest[: nz - 1], rest[nz - 1 : 2 * nz - 2]
    w_ref, out_ref, x, acc, sems = rest[2 * nz - 2 :]
    b = pl.program_id(0)
    n, _, depth, columns = w_ref.shape
    depth = depth // 3
    width = x.shape[1]

    @pl.when(b == 0)
    def _():
        in_order(nz, info[Z], own, rights, lefts, x, sems)
        acc[...] = jnp.zeros(acc.shape, F32)

    gate = nn(x[...], w_ref[:, 0, 0:depth].reshape(width, columns))
    up = nn(x[...], w_ref[:, 0, depth : 2 * depth].reshape(width, columns))
    active = (gate / (1.0 + jnp.exp(-gate)) * up).astype(BF16)
    if depth == UNIT:
        for r in range(n):
            at = slice(r * depth, (r + 1) * depth)
            acc[:, at] += nn(active, w_ref[r, 0, 2 * depth :])
    else:
        acc[...] += nt(active, w_ref[:, 0, 2 * depth :].reshape(width, columns))

    @pl.when(b == pl.num_programs(0) - 1)
    def _():
        out_ref[...] = acc[...].astype(BF16).reshape(out_ref.shape)


def peak_kernel(info, every, vocab, out):
    b = pl.program_id(0)
    best = jnp.max(nt(vocab[...], every[...]), axis=0, keepdims=True)
    best = jnp.broadcast_to(best, (out.shape[0], every.shape[0]))

    @pl.when(b == 0)
    def _():
        out[...] = jnp.zeros(out.shape, F32)
        out[:, : every.shape[0]] = best

    @pl.when(b > 0)
    def _():
        out[:, : every.shape[0]] = jnp.maximum(out[:, : every.shape[0]], best)


def reduce_to_owners(parts, z, nz):
    def take(index):
        return lax.dynamic_index_in_dim(parts, jnp.clip(index, 0, nz - 1), 0, keepdims=False)

    came = None
    for s in range(1, nz):
        right, left = take(nz - s + z), take(s + z - nz)
        if came is not None:
            right, left = right + came[0], left + came[1]
        came = (
            lax.ppermute(right, "mlp", [(i, i + 1) for i in range(s)]),
            lax.ppermute(left, "mlp", [(nz - 1 - i, nz - 2 - i) for i in range(s)]),
        )
    return came


def spread(own, nz):
    rights, lefts = [own], [own]
    for s in range(1, nz):
        rights.append(lax.ppermute(rights[-1], "mlp", [(i, i + 1) for i in range(s - 1, nz - 1)]))
        lefts.append(lax.ppermute(lefts[-1], "mlp", [(i + 1, i) for i in range(0, nz - s)]))
    return rights[1:] + lefts[1:]


def butterfly(values, combine, n, nz, low=1):
    bit = low
    while bit < n * nz:
        if bit < n:
            axis, pairs = "req", [(i, i ^ bit) for i in range(n)]
        else:
            axis, pairs = "mlp", [(i, i ^ (bit // n)) for i in range(nz)]
        values = combine(values, lax.ppermute(values, axis, pairs))
        bit *= 2
    return values


def layer(sizes, sizes_n, table_rows, info, hidden, gains, w_qkv, w_out, w_gateup, w_down, picked, vocab):
    n, nz = sizes_n
    z = lax.axis_index("mlp")
    gain_attn, gain_mlp, final_gain = gains
    slots, length, width = hidden.shape
    rows, half = slots * length, length // 2
    columns = w_qkv.shape[2]
    units = w_down.shape[0]
    slots_all = n * slots
    swap = [(i, i ^ 1) for i in range(n)]
    factor_shape = picked[0].shape
    received = [picked[0]] + [
        lax.ppermute(picked[j], "req", [(i, i ^ j) for i in range(n)]) for j in range(1, n)
    ]

    cosine, sine = rope_tables(length)
    part_rows = slots * half
    projected = []
    for h in range(2):
        table = pl.BlockSpec((half, 128), lambda i, _, h=h: (h, 0))
        projected.append(
            call(
                project_kernel,
                (1,),
                [
                    pl.BlockSpec((slots, half, width), lambda i, _, h=h: (0, h, 0)),
                    whole((1, width)),
                    whole(w_qkv.shape),
                    table,
                    table,
                ],
                [whole((part_rows, columns))] * 3 + [whole((part_rows, width))],
                [
                    jax.ShapeDtypeStruct((part_rows, columns), BF16),
                    jax.ShapeDtypeStruct((part_rows, columns), BF16),
                    jax.ShapeDtypeStruct((part_rows, columns), F32),
                    jax.ShapeDtypeStruct((part_rows, width), BF16),
                ],
                flops=2 * part_rows * width * 3 * columns,
                nbytes=2 * (2 * part_rows * width + 3 * width * columns),
            )(info, hidden, gain_attn, w_qkv, cosine, sine)
        )

    quarters = [size // nz for size in sizes]
    quarter_shapes = [jax.ShapeDtypeStruct((q, width), BF16) for q in quarters]
    quarter_specs = [whole((q, width)) for q in quarters]
    shared = call(
        functools.partial(hidden_kernel, slots, nz, sizes),
        (1,),
        [whole((rows, width))],
        quarter_specs * 2,
        quarter_shapes * 2,
        flops=4 * sum(quarters) * rows * width,
        nbytes=2 * rows * width,
    )(info, hidden.reshape(rows, width))
    hidden_own = shared[:2]
    hidden_other = [lax.ppermute(piece, "req", swap) for piece in shared[2:]]

    depth = w_down.shape[1]
    merged = call(
        merge_kernel,
        (1,),
        [whole(w_gateup.shape), whole(w_down.shape), ANY],
        whole((units // UNIT, 3 * depth, UNIT)),
        jax.ShapeDtypeStruct((units // UNIT, 3 * depth, UNIT), BF16),
        nbytes=12 * depth * units,
    )(info, w_gateup, w_down, projected[0][1])
    weights = lax.all_gather(merged, "req", axis=0)

    attended, other = [], []
    for h in range(2):
        by_slot = lambda w: pl.BlockSpec((half, w), lambda s, _: (s, 0))
        table = pl.BlockSpec((half, 128), lambda s, _, h=h: (h, 0))
        attended.append(
            call(
                functools.partial(attend_kernel, slots, table_rows, n, h),
                (slots,),
                [ANY, ANY, by_slot(columns), by_slot(width), table, table]
                + [by_slot(columns)] * (2 * h + 2)
                + [whole(factor_shape)] * n,
                by_slot(columns),
                jax.ShapeDtypeStruct((part_rows, columns), BF16),
                [pltpu.VMEM((half, columns), BF16), pltpu.VMEM(factor_shape[1:], BF16)],
                flops=8 * part_rows * (h + 1) * half * columns,
                nbytes=2 * part_rows * (width + 6 * columns),
            )(
                info,
                *((projected[1][1], shared[0]) if h == 0 else (attended[0], merged)),
                projected[h][2],
                projected[h][3],
                cosine,
                sine,
                *[projected[i][0] for i in range(h + 1)],
                *[projected[i][1] for i in range(h + 1)],
                *received,
            )
        )
        other.append(lax.ppermute(attended[h], "req", swap))

    def own_part(q):
        return pl.BlockSpec((1, q, width), lambda i, info: (info[Z], 0, 0))

    out, sums, lasts = None, [], None
    for h in range(2):
        q, size, spec = quarters[h], sizes[h], quarter_specs[h]
        part_shape = jax.ShapeDtypeStruct((nz, q, width), BF16)
        parts = [attended[h], other[h]] + ([attended[0], other[0]] if h == 1 else [])
        head_parts = call(
            functools.partial(mix_kernel, slots, size, h),
            (1,),
            [ANY, whole(w_out.shape)] + [whole((part_rows, columns))] * len(parts),
            whole(part_shape.shape),
            part_shape,
            flops=2 * size * columns * (2 * part_rows + width),
            nbytes=2 * (columns * (2 * part_rows + width) + size * width),
        )(info, attended[1], w_out, *parts)
        right, left = reduce_to_owners(head_parts, z, nz)
        stream, mid = call(
            stream_kernel,
            (1,),
            [own_part(q)] + [spec] * 4 + [whole((1, width))],
            [spec, spec],
            [quarter_shapes[h]] * 2,
            nbytes=14 * q * width,
        )(info, head_parts, right, left, hidden_own[h], hidden_other[h], gain_mlp)
        unit_parts = call(
            functools.partial(unit_kernel, nz),
            (units // UNIT,),
            [ANY] * (2 * nz - 1)
            + [pl.BlockSpec((n, 1) + weights.shape[2:], lambda b, _: (0, b, 0, 0))],
            whole(part_shape.shape),
            part_shape,
            [
                pltpu.VMEM((size, width), BF16),
                pltpu.VMEM((size, width), F32),
                pltpu.SemaphoreType.DMA((nz,)),
            ],
            flops=6 * size * width * units,
            nbytes=2 * weights.size,
        )(info, mid, *spread(mid, nz), weights)
        right, left = reduce_to_owners(unit_parts, z, nz)
        extra = [(slots_all, width)] if h == 1 else []
        finished = call(
            functools.partial(finish_kernel, slots, size, h),
            (1,),
            [own_part(q)] + [spec] * 3 + [whole((1, width))],
            [spec, whole((8, 128))] + [whole(e) for e in extra],
            [quarter_shapes[h], jax.ShapeDtypeStruct((8, 128), F32)]
            + [jax.ShapeDtypeStruct(e, BF16) for e in extra],
            nbytes=10 * q * width,
        )(info, unit_parts, right, left, stream, final_gain)
        sums.append(finished[1])
        lasts = finished[2:]
        mine = call(
            functools.partial(order_kernel, nz),
            (1,),
            [ANY] * (2 * nz - 1),
            whole((size, width)),
            jax.ShapeDtypeStruct((size, width), BF16),
            [pltpu.SemaphoreType.DMA((nz,))],
            nbytes=4 * size * width,
        )(info, finished[0], *spread(finished[0], nz))
        theirs = lax.ppermute(mine, "req", swap)
        held = [] if out is None else [out]
        out = call(
            functools.partial(unpack_kernel, slots, h),
            (slots,),
            [ANY, ANY] + [ANY] * len(held),
            pl.BlockSpec((half, width), lambda s, _, h=h: (2 * s + h, 0)),
            jax.ShapeDtypeStruct((rows, width), BF16),
            [pltpu.VMEM((2 * size + half, width), BF16), pltpu.SemaphoreType.DMA((2,))],
            nbytes=2 * rows * width,
            aliases={3: 0} if held else None,
        )(info, mine, theirs, *held)

    every = butterfly(lasts[0], lambda a, b: a + b, n, nz)
    block = vocab.shape[0] // 3
    peaks = call(
        peak_kernel,
        (3,),
        [whole(every.shape), pl.BlockSpec((block, width), lambda b, _: (b, 0))],
        whole((8, 128)),
        jax.ShapeDtypeStruct((8, 128), F32),
        flops=2 * slots_all * vocab.size,
        nbytes=2 * vocab.size,
    )(info, every, vocab)
    both = jnp.concatenate([sums[0] + sums[1], peaks], axis=0)

    def combine(a, b):
        row = lax.broadcasted_iota(jnp.int32, a.shape, 0)
        return jnp.where(row < 8, a + b, jnp.maximum(a, b))

    both = butterfly(both, combine, n, nz)
    return out.reshape(slots, length, width), both


def per_device(sizes_n, *arrays):
    (hidden, lengths, slot_request, adapter_of, adapter_slot, gain_attn, gain_mlp, final_gain) = (
        arrays[:8]
    )
    (w_qkv, w_out, w_gateup, w_down, adapter_down, adapter_up, vocab) = arrays[8:]
    n, nz = sizes_n
    slots, length, width = hidden.shape
    me, z = lax.axis_index("req"), lax.axis_index("mlp")
    part_rows = slots * length // 2
    classes = [
        (part_rows * a // 8, part_rows * b // 8 + c) for a, b, c in CLASSES
    ]
    factor_shape = (slots, adapter_down.shape[1], width + adapter_up.shape[2])
    info, *picked = pl.pallas_call(
        functools.partial(setup_kernel, slots, length // 2, classes),
        in_specs=[SMEM] * 6 + [pl.BlockSpec(memory_space=pltpu.VMEM)] * 2,
        out_specs=[SMEM] + [pl.BlockSpec(memory_space=pltpu.VMEM)] * n,
        out_shape=[jax.ShapeDtypeStruct((TABLES + 9 * slots,), jnp.int32)]
        + [jax.ShapeDtypeStruct(factor_shape, BF16)] * n,
        compiler_params=pltpu.CompilerParams(vmem_limit_bytes=VMEM_LIMIT),
    )(
        me.reshape(1), z.reshape(1), lengths, slot_request, adapter_of, adapter_slot,
        adapter_down, adapter_up,
    )
    operands = (
        info,
        hidden,
        tuple(g.reshape(1, width) for g in (gain_attn, gain_mlp, final_gain)),
        w_qkv.transpose(1, 0, 2),
        w_out,
        w_gateup,
        w_down,
        tuple(picked),
        vocab,
    )
    branches = [
        functools.partial(layer, sizes, sizes_n, adapter_down.shape[0]) for sizes in classes
    ]
    if len(branches) == 1:
        out, both = branches[0](*operands)
    else:
        out, both = lax.switch(info[CLASS], branches, *operands)
    slots_all = slot_request.shape[0]
    norm_sums, peaks = both[0, :slots_all], both[8, :slots_all]
    requests = jnp.arange(slots_all, dtype=jnp.int32)
    owners = slot_request[None, :] == requests[:, None]
    norm_sums = jnp.sum(jnp.where(owners, norm_sums[None, :], 0.0), axis=1)
    request_norm = jnp.sqrt(norm_sums / (lengths.astype(F32) * width))
    request_peak = jnp.sum(jnp.where(owners, peaks[None, :], 0.0), axis=1)
    return out, request_norm, request_peak


def solution(mesh):
    return jax.shard_map(
        functools.partial(per_device, (mesh.shape["req"], mesh.shape["mlp"])),
        mesh=mesh,
        in_specs=(
            P("req", None, None),
            P(),
            P(),
            P(),
            P(),
            P(),
            P(),
            P(),
            P(None, None, "mlp"),
            P("mlp", None),
            P("req", None, "mlp"),
            P("mlp", "req"),
            P("req", None, None),
            P("req", None, "mlp"),
            P(("req", "mlp"), None),
        ),
        out_specs=(P("req", None, None), P(), P()),
        check_vma=False,
    )
```

```python
import functools
import math

import jax
import jax.numpy as jnp
import numpy as np
from jax import lax
from jax.experimental import pallas as pl
from jax.experimental.pallas import tpu as pltpu
from jax.sharding import PartitionSpec as P

HEAD_WIDTH = 64
EPSILON = 1e-05
ROPE_BASE = 130000.0
ADAPTER_SCALE = 2.0
MASKED = -1e30
F32, BF16 = jnp.float32, jnp.bfloat16
UNIT = 256
CLASSES = [(7, 4, 0), (7, 5, 0), (8, 4, 0), (8, 5, 0), (8, 6, 0), (8, 8, 64)]
MIB = 1024 * 1024

ME, Z, CORE, CLASS, TABLES = 0, 1, 2, 3, 8
LAST_ROWS = 16
ANY = pl.BlockSpec(memory_space=pl.ANY)
SMEM = pl.BlockSpec(memory_space=pltpu.SMEM)


def nt(a, b):
    return lax.dot_general(a, b, (((1,), (1,)), ((), ())), preferred_element_type=F32)


def nn(a, b):
    return jnp.dot(a, b, preferred_element_type=F32)


def call(
    kernel, grid, ins, outs, shapes, scratch=(), flops=0, nbytes=0, aliases=None, vmem=16
):
    spec = pltpu.PrefetchScalarGridSpec(
        num_scalar_prefetch=1, grid=grid, in_specs=ins, out_specs=outs, scratch_shapes=scratch
    )
    return pl.pallas_call(
        kernel,
        grid_spec=spec,
        out_shape=shapes,
        input_output_aliases=aliases or {},
        compiler_params=pltpu.CompilerParams(vmem_limit_bytes=vmem * MIB),
        cost_estimate=pl.CostEstimate(
            flops=int(flops), bytes_accessed=int(nbytes), transcendentals=0
        ),
    )


def whole(shape):
    zeros = (0,) * len(shape)
    return pl.BlockSpec(tuple(shape), lambda *_: zeros)


def rope_tables(length):
    half = HEAD_WIDTH // 2
    frequency = np.float32(ROPE_BASE) ** (-(np.arange(half, dtype=np.float32) * 2.0 / HEAD_WIDTH))
    angles = np.arange(length, dtype=np.float32)[:, None] * frequency.astype(np.float32)[None, :]
    angles = angles.astype(np.float32)
    cosine, sine = np.cos(angles), np.sin(angles)
    return (
        np.concatenate([cosine] * 4, axis=1).astype(np.float32),
        np.concatenate([-sine, sine, -sine, sine], axis=1).astype(np.float32),
    )


def rotate(block, cosine, sine):
    lane = lax.broadcasted_iota(jnp.int32, block.shape, 1)
    front = (lane % HEAD_WIDTH) < HEAD_WIDTH // 2
    partner = jnp.where(
        front, pltpu.roll(block, 128 - HEAD_WIDTH // 2, 1), pltpu.roll(block, HEAD_WIDTH // 2, 1)
    )
    return block * cosine + partner * sine


def live_at(slots, h, g):
    return TABLES + slots + h * 4 * slots + g


def place_at(slots, h, g):
    return TABLES + slots + h * 4 * slots + 2 * slots + g


def setup_kernel(
    slots, half, classes, me_ref, z_ref, lengths, slot_request, adapter_of, adapter_slot, down, up,
    info, *outs
):
    table_rows, _, width = down.shape
    me, z = me_ref[0], z_ref[0]
    core, chip = lax.rem(me, 2), lax.div(me, 2)
    chip_slots = 2 * slots
    info[ME], info[Z], info[CORE] = me, z, core

    def split(slot):
        live = lengths[slot_request[slot]]
        first = jnp.minimum(live, half)
        return first, live - first

    def aligned(live):
        return lax.div(live + 15, 16) * 16

    most = [jnp.int32(0), jnp.int32(0)]
    for c in range(slot_request.shape[0] // chip_slots):
        total = [jnp.int32(0), jnp.int32(LAST_ROWS)]
        for g in range(chip_slots):
            for h, live in enumerate(split(c * chip_slots + g)):
                total[h] = total[h] + aligned(live)
        most = [jnp.maximum(most[h], total[h]) for h in range(2)]
    choice = jnp.int32(len(classes) - 1)
    for i in reversed(range(len(classes) - 1)):
        fits = (most[0] <= 2 * classes[i][0]) & (most[1] <= 2 * classes[i][1])
        choice = jnp.where(fits, i, choice)
    info[CLASS] = choice
    total = [jnp.int32(0), jnp.int32(LAST_ROWS)]
    for g in range(chip_slots):
        for h, live in enumerate(split(chip * chip_slots + g)):
            info[live_at(slots, h, g)] = live
            info[place_at(slots, h, g)] = total[h]
            total[h] = total[h] + aligned(live)
    for s in range(slots):
        info[TABLES + s] = adapter_slot[adapter_of[slot_request[me * slots + s]]]
    for j, out in enumerate(outs):
        for s in range(slots):
            slot = (me ^ j) * slots + s
            row = lax.rem(adapter_slot[adapter_of[slot_request[slot]]], table_rows)
            out[s, :, :width] = down[row]
            out[s, :, width:] = up[row]


def merge_kernel(info, gate_up, down, out):
    depth, units = down.shape[1], down.shape[0]
    for b in range(units // UNIT):
        at = slice(b * UNIT, (b + 1) * UNIT)
        out[b, 0:depth] = gate_up[:, 0, at]
        out[b, depth : 2 * depth] = gate_up[:, 1, at]
        out[b, 2 * depth :] = down[at, :] if depth == UNIT else down[at, :].T


def project_kernel(
    info, x_ref, gain_ref, w_ref, cos_ref, sin_ref, k_ref, v_ref, q_ref, normed_ref
):
    slots, rows, width = x_ref.shape
    group = 64
    for s in range(slots):
        for i in range(rows // group):
            x = x_ref[s, i * group : (i + 1) * group].astype(F32)
            mean = jnp.mean(x * x, axis=-1, keepdims=True)
            at = slice(s * rows + i * group, s * rows + (i + 1) * group)
            normed_ref[at] = (x * lax.rsqrt(mean + EPSILON) * gain_ref[...]).astype(BF16)
    product = nn(normed_ref[...], w_ref[1])
    for s in range(slots):
        at = slice(s * rows, (s + 1) * rows)
        for g in range(product.shape[1] // 128):
            lanes = slice(g * 128, g * 128 + 128)
            k_ref[at, lanes] = rotate(product[at, lanes], cos_ref[...], sin_ref[...]).astype(BF16)
    v_ref[...] = nn(normed_ref[...], w_ref[2]).astype(BF16)
    q_ref[...] = nn(normed_ref[...], w_ref[0])


def attend_kernel(slots, table_rows, n, h, info, q_ref, normed_ref, cos_ref, sin_ref, *rest):
    keys, values = rest[: h + 1], rest[h + 1 : 2 * h + 2]
    received, (out_ref, queries) = rest[2 * h + 2 : 2 * h + 2 + (n if h == 0 else 1)], rest[-2:]
    s = pl.program_id(0)
    length, columns = q_ref.shape
    width = normed_ref.shape[1]
    if h == 0:
        out_ref, picked, queries, sem = rest[-4:]
        factors = picked.at[0]
        source = info[ME] ^ lax.div(info[TABLES + s], table_rows)
        for j in range(n):

            @pl.when(source == j)
            def _(j=j):
                pltpu.make_async_copy(received[j].at[s], factors, sem.at[0]).start()

        pltpu.make_async_copy(received[0].at[s], factors, sem.at[0]).wait()
    else:
        factors = received[0].at[0]
    low_rank = nt(normed_ref[...], factors[:, :width]).astype(BF16)
    raised = nn(low_rank, factors[:, width:])
    full = q_ref[...] + ADAPTER_SCALE * raised
    for g in range(columns // 128):
        lanes = slice(g * 128, g * 128 + 128)
        queries[:, lanes] = rotate(full[:, lanes], cos_ref[...], sin_ref[...]).astype(BF16)
    step = length
    scale = HEAD_WIDTH ** (-0.5) * math.log2(math.e)

    def pair(g):
        lanes = slice(g * 128, g * 128 + 128)
        for b in range(length // step):
            end = (b + 1) * step
            q = queries[b * step : end, lanes]
            first = lax.broadcasted_iota(jnp.int32, q.shape, 1) < HEAD_WIDTH
            zero = jnp.zeros_like(q)
            both = jnp.concatenate([jnp.where(first, q, zero), jnp.where(first, zero, q)], axis=0)
            scores = nt(both, keys[h][0:end, lanes]) * scale
            row = lax.broadcasted_iota(jnp.int32, scores.shape, 0) % step + b * step
            col = lax.broadcasted_iota(jnp.int32, scores.shape, 1)
            scores = [jnp.where(col <= row, scores, MASKED)]
            used = [values[h][0:end, lanes]]
            for before in range(h):
                scores.append(nt(both, keys[before][:, lanes]) * scale)
                used.append(values[before][:, lanes])
            top = functools.reduce(
                jnp.maximum, [jnp.max(part, axis=1, keepdims=True) for part in scores]
            )
            weights = [jnp.exp2(part - top) for part in scores]
            total = sum(jnp.sum(part, axis=1, keepdims=True) for part in weights)
            mixed = sum(nn(part.astype(BF16), value) for part, value in zip(weights, used))
            mixed = mixed / total
            out_ref[b * step : end, lanes] = jnp.where(first, mixed[:step], mixed[step:]).astype(
                BF16
            )

    for g in range(columns // 128):
        pair(g)


def targets(info, row, slots, h, half, core, stride, start):
    place = jnp.full(row.shape, -1, jnp.int32)
    for s in range(slots):
        g = core * slots + s
        live = info[live_at(slots, h, g)]
        at = info[place_at(slots, h, g)]
        inside = (row >= at) & (row < at + live)
        place = jnp.where(inside, row - at + s * stride + start, place)
    return place


def last_targets(info, row, slots, half, core, h, stride, start):
    place = jnp.full(row.shape, -1, jnp.int32)
    for s in range(slots):
        g = core * slots + s
        second = info[live_at(slots, 1, g)]
        live = info[live_at(slots, 0, g)] if h == 0 else second
        there = (second > 0) if h == 1 else (second == 0)
        place = jnp.where((row == g) & there, s * stride + start + live - 1, place)
    return place


def one_hot(place, columns):
    col = lax.broadcasted_iota(jnp.int32, (place.shape[0], columns), 1)
    return jnp.where(col == place, 1.0, 0.0).astype(BF16)


def hidden_kernel(slots, nz, sizes, info, hidden_ref, *outs):
    count = len(sizes)
    tokens = hidden_ref.shape[0]
    length = tokens // slots
    half = length // 2
    core = info[CORE]
    for h in range(count):
        quarter = sizes[h] // nz
        for whose in range(2):
            target_core = core if whose == 0 else 1 - core
            base = target_core * sizes[h] + info[Z] * quarter
            row = lax.broadcasted_iota(jnp.int32, (quarter, 1), 0) + base
            place = targets(info, row, slots, h, half, core, length, h * half)
            if h == 1:
                for part in range(2):
                    late = last_targets(info, row, slots, half, core, part, length, part * half)
                    place = jnp.maximum(place, late)
            outs[whose * count + h][...] = nn(one_hot(place, tokens), hidden_ref[...]).astype(BF16)


def mix_kernel(slots, size, h, info, w_ref, *rest):
    parts, out_ref = rest[:-1], rest[-1]
    tokens = parts[0].shape[0]
    half = tokens // slots
    core = info[CORE]
    cores = (core, 1 - core)
    row = lax.broadcasted_iota(jnp.int32, (size, 1), 0) + core * size
    packed = 0.0
    for whose in range(2):
        place = targets(info, row, slots, h, half, cores[whose], half, 0)
        if h == 1:
            late = last_targets(info, row, slots, half, cores[whose], 1, half, 0)
            place = jnp.maximum(place, late)
        packed = packed + nn(one_hot(place, tokens), parts[whose][...])
    if h == 1:
        front = 0.0
        for whose in range(2):
            place = last_targets(info, row[:LAST_ROWS], slots, half, cores[whose], 0, half, 0)
            front = front + nn(one_hot(place, tokens), parts[2 + whose][...])
        packed = jnp.concatenate([packed[:LAST_ROWS] + front, packed[LAST_ROWS:]], axis=0)
    product = nn(packed.astype(BF16), w_ref[...]).astype(BF16)
    out_ref[...] = product.reshape(out_ref.shape)


def stream_kernel(info, own, other, gain, *rest):
    terms, (stream_ref, normed_ref) = rest[:-2], rest[-2:]
    mixed = sum(term[...].astype(F32) for term in terms)
    hidden = own[...].astype(F32) + other[...].astype(F32)
    stream = (hidden + mixed).astype(BF16)
    stream_ref[...] = stream
    x = stream.astype(F32)
    mean = jnp.mean(x * x, axis=-1, keepdims=True)
    normed_ref[...] = (x * lax.rsqrt(mean + EPSILON) * gain[...]).astype(BF16)


def finish_kernel(slots, size, h, count, info, stream, gain, *rest):
    terms, (out_ref, sums_ref), lasts = rest[:count], rest[count : count + 2], rest[count + 2 :]
    quarter, width = stream.shape
    chip_slots = 2 * slots
    total = sum(term[...].astype(F32) for term in terms)
    result = stream[...].astype(F32) + total
    base = info[CORE] * size + info[Z] * quarter
    row = lax.broadcasted_iota(jnp.int32, (quarter, 1), 0) + base
    keep = (row < chip_slots) if h == 1 else (row < 0)
    belongs = []
    for g in range(chip_slots):
        live, at = info[live_at(slots, h, g)], info[place_at(slots, h, g)]
        inside = (row >= at) & (row < at + live)
        belongs.append(inside)
        keep = keep | inside
    rounded = jnp.where(keep, result, 0.0).astype(BF16)
    out_ref[...] = rounded
    wide = rounded.astype(F32)
    squares = jnp.sum(wide * wide, axis=1, keepdims=True)
    lane = lax.broadcasted_iota(jnp.int32, sums_ref.shape, 1)
    first_slot = lax.div(info[ME], 2) * chip_slots
    sums = jnp.zeros(sums_ref.shape, F32)
    for g in range(chip_slots):
        part = jnp.sum(jnp.where(belongs[g], squares, 0.0))
        sums = jnp.where(lane == first_slot + g, part, sums)
    sums_ref[...] = sums
    for last_ref in lasts:
        last_ref[...] = jnp.zeros(last_ref.shape, BF16)
        front = wide[:LAST_ROWS]
        mean = jnp.mean(front * front, axis=-1, keepdims=True)
        last = (front * lax.rsqrt(mean + EPSILON) * gain[...]).astype(BF16)
        slot = lax.broadcasted_iota(jnp.int32, (last_ref.shape[0], LAST_ROWS), 0) - first_slot
        kept = lax.broadcasted_iota(jnp.int32, slot.shape, 1)
        pick = jnp.where((slot == kept) & (kept < chip_slots), 1.0, 0.0).astype(BF16)

        @pl.when(base == 0)
        def _():
            last_ref[...] = nn(pick, last).astype(BF16)


def in_order(nz, z, own, rights, lefts, out, sems):
    quarter = own.shape[0]

    def copy(piece, place):
        return pltpu.make_async_copy(
            piece, out.at[pl.ds(place * quarter, quarter)], sems.at[place]
        )

    for place in range(nz):

        @pl.when(z == place)
        def _(place=place):
            copy(own, place).start()

        for d in range(1, nz):

            @pl.when(z - place == d)
            def _(place=place, d=d):
                copy(rights[d - 1], place).start()

            @pl.when(place - z == d)
            def _(place=place, d=d):
                copy(lefts[d - 1], place).start()

    for place in range(nz):
        copy(own, place).wait()


def order_kernel(nz, info, own, *rest):
    rights, lefts, (out, sems) = rest[: nz - 1], rest[nz - 1 : 2 * nz - 2], rest[2 * nz - 2 :]
    in_order(nz, info[Z], own, rights, lefts, out, sems)


def unpack_kernel(slots, h, info, mine, theirs, *rest):
    out, packed, sems = rest[-3:]
    s = pl.program_id(0)
    size = mine.shape[0]
    core = info[CORE]

    @pl.when(s == 0)
    def _():
        copies = [
            pltpu.make_async_copy(
                piece,
                packed.at[pl.ds(pl.multiple_of(place * size, 16), size)],
                sems.at[i],
            )
            for i, (piece, place) in enumerate(((mine, core), (theirs, 1 - core)))
        ]
        for copy in copies:
            copy.start()
        for copy in copies:
            copy.wait()

    g = core * slots + s
    live, at = info[live_at(slots, h, g)], info[place_at(slots, h, g)]
    rows = packed[pl.ds(pl.multiple_of(at, 16), out.shape[0])]
    row = lax.broadcasted_iota(jnp.int32, (out.shape[0], 1), 0)
    out[...] = jnp.where(row < live, rows, jnp.zeros((), BF16))


def unit_kernel(nz, info, own, *rest):
    rights, lefts = rest[: nz - 1], rest[nz - 1 : 2 * nz - 2]
    w_ref, out_ref, x, acc, sems = rest[2 * nz - 2 :]
    b = pl.program_id(0)
    n, _, depth, columns = w_ref.shape
    depth = depth // 3
    width = x.shape[1]

    @pl.when(b == 0)
    def _():
        in_order(nz, info[Z], own, rights, lefts, x, sems)
        acc[...] = jnp.zeros(acc.shape, F32)

    gate = nn(x[...], w_ref[:, 0, 0:depth].reshape(width, columns))
    up = nn(x[...], w_ref[:, 0, depth : 2 * depth].reshape(width, columns))
    active = (gate / (1.0 + jnp.exp(-gate)) * up).astype(BF16)
    if depth == UNIT:
        for r in range(n):
            at = slice(r * depth, (r + 1) * depth)
            acc[:, at] += nn(active, w_ref[r, 0, 2 * depth :])
    else:
        acc[...] += nt(active, w_ref[:, 0, 2 * depth :].reshape(width, columns))

    @pl.when(b == pl.num_programs(0) - 1)
    def _():
        out_ref[...] = acc[...].astype(BF16).reshape(out_ref.shape)


def peak_kernel(info, every, vocab, out):
    b = pl.program_id(0)
    best = jnp.max(nt(vocab[...], every[...]), axis=0, keepdims=True)
    best = jnp.broadcast_to(best, (out.shape[0], every.shape[0]))

    @pl.when(b == 0)
    def _():
        out[...] = jnp.zeros(out.shape, F32)
        out[:, : every.shape[0]] = best

    @pl.when(b > 0)
    def _():
        out[:, : every.shape[0]] = jnp.maximum(out[:, : every.shape[0]], best)


def following(info, array):
    return lax.optimization_barrier((info, array))[0]


class Order:
    def __init__(self):
        self.before = None

    def __call__(self, *arrays):
        if self.before is not None:
            *arrays, _ = lax.optimization_barrier((*arrays, self.before))
        elif len(arrays) > 1:
            arrays = lax.optimization_barrier(arrays)
        self.before = arrays[0]
        return arrays


def reduce_start(parts, order, z, nz):
    last = nz - 1
    index = jnp.where(z == 0, last, 0)
    (message,) = order(lax.dynamic_index_in_dim(parts, index, 0, keepdims=False))
    came = lax.ppermute(message, "mlp", [(0, 1), (last, last - 1)])
    return message, [came, came]


def reduce_step(parts, came, s, order, z, nz):
    def take(index):
        return lax.dynamic_index_in_dim(parts, jnp.clip(index, 0, nz - 1), 0, keepdims=False)

    last = nz - 1
    *came, _ = lax.optimization_barrier((*came, order.before))
    right, left = take(nz - s + z), take(s + z - nz)
    if s == 2:
        right = jnp.where(z == 0, right, right + came[0])
        left = jnp.where(z == last, left, left + came[1])
    else:
        right, left = right + came[0], left + came[1]
    right, left = order(right, left)
    return [
        lax.ppermute(right, "mlp", [(i, i + 1) for i in range(s)]),
        lax.ppermute(left, "mlp", [(last - i, last - 1 - i) for i in range(s)]),
    ]


def spread_step(rights, lefts, s, order, z, nz):
    last = nz - 1
    if s < last:
        right, left = order(rights[-1], lefts[-1])
        rights.append(lax.ppermute(right, "mlp", [(i, i + 1) for i in range(s - 1, last)]))
        lefts.append(lax.ppermute(left, "mlp", [(i + 1, i) for i in range(0, nz - s)]))
    else:
        (message,) = order(jnp.where(z == last - 1, rights[-1], lefts[-1]))
        message = lax.ppermute(message, "mlp", [(last - 1, last), (1, 0)])
        rights.append(message)
        lefts.append(message)


def hops(n, nz):
    bit = 2
    while bit < n * nz:
        if bit < n:
            yield "req", [(i, i ^ bit) for i in range(n)]
        else:
            yield "mlp", [(i, i ^ (bit // n)) for i in range(nz)]
        bit *= 2
    yield "req", [(i, i ^ 1) for i in range(n)]


def layer(sizes, sizes_n, table_rows, info, hidden, gains, w_qkv, w_out, w_gateup, w_down, picked, vocab):
    n, nz = sizes_n
    z = lax.axis_index("mlp")
    gain_attn, gain_mlp, final_gain = gains
    slots, length, width = hidden.shape
    rows, half = slots * length, length // 2
    columns = w_qkv.shape[2]
    units = w_down.shape[0]
    slots_all = n * slots
    swap = [(i, i ^ 1) for i in range(n)]
    factor_shape = picked[0].shape
    received = [picked[0]] + [
        lax.ppermute(picked[j], "req", [(i, i ^ j) for i in range(n)]) for j in range(1, n)
    ]

    cosine, sine = rope_tables(length)
    part_rows = slots * half
    projected = []
    for h in range(2):
        table = pl.BlockSpec((half, 128), lambda i, _, h=h: (h, 0))
        projected.append(
            call(
                project_kernel,
                (1,),
                [
                    pl.BlockSpec((slots, half, width), lambda i, _, h=h: (0, h, 0)),
                    whole((1, width)),
                    whole(w_qkv.shape),
                    table,
                    table,
                ],
                [whole((part_rows, columns))] * 3 + [whole((part_rows, width))],
                [
                    jax.ShapeDtypeStruct((part_rows, columns), BF16),
                    jax.ShapeDtypeStruct((part_rows, columns), BF16),
                    jax.ShapeDtypeStruct((part_rows, columns), F32),
                    jax.ShapeDtypeStruct((part_rows, width), BF16),
                ],
                vmem=32,
                flops=2 * part_rows * width * 3 * columns,
                nbytes=2 * (2 * part_rows * width + 3 * width * columns),
            )(info, hidden, gain_attn, w_qkv, cosine, sine)
        )

    quarters = [size // nz for size in sizes]
    quarter_shapes = [jax.ShapeDtypeStruct((q, width), BF16) for q in quarters]
    quarter_specs = [whole((q, width)) for q in quarters]
    attended, other, head_parts, came, order = [], [], [], [], Order()
    for h in range(2):
        by_slot = lambda w: pl.BlockSpec((half, w), lambda s, _: (s, 0))
        table = pl.BlockSpec((half, 128), lambda s, _, h=h: (h, 0))
        by_factor = pl.BlockSpec((1,) + factor_shape[1:], lambda s, _: (s, 0, 0))
        own_factors = h == 0
        mixed = call(
            functools.partial(attend_kernel, slots, table_rows, n, h),
            (slots,),
            [by_slot(columns), by_slot(width), table, table]
            + [by_slot(columns)] * (2 * h + 2)
            + ([ANY] * n if own_factors else [by_factor]),
            [by_slot(columns)] + [by_factor] * own_factors,
            [jax.ShapeDtypeStruct((part_rows, columns), BF16)]
            + [jax.ShapeDtypeStruct(factor_shape, BF16)] * own_factors,
            [pltpu.VMEM((half, columns), BF16)] + [pltpu.SemaphoreType.DMA((1,))] * own_factors,
            flops=8 * part_rows * (h + 1) * half * columns,
            nbytes=2 * part_rows * (width + 6 * columns),
        )(
            following(info, projected[1][1] if own_factors else first),
            projected[h][2],
            projected[h][3],
            cosine,
            sine,
            *[projected[i][0] for i in range(h + 1)],
            *[projected[i][1] for i in range(h + 1)],
            *received,
        )
        attended.append(mixed[0])
        if own_factors:
            received = mixed[1:]
        other.append(lax.ppermute(attended[h], "req", swap))
        size, q = sizes[h], quarters[h]
        part_shape = jax.ShapeDtypeStruct((nz, q, width), BF16)
        parts = [attended[h], other[h]] + ([attended[0], other[0]] if h == 1 else [])
        mixed = call(
            functools.partial(mix_kernel, slots, size, h),
            (1,),
            [whole(w_out.shape)] + [whole((part_rows, columns))] * len(parts),
            whole(part_shape.shape),
            part_shape,
            vmem=24,
            flops=2 * size * columns * (2 * part_rows + width),
            nbytes=2 * (columns * (2 * part_rows + width) + size * width),
        )(info, w_out, *parts)
        head_parts.append(mixed)
        first, came_h = reduce_start(mixed, order, z, nz)
        came.append(came_h)

    depth = w_down.shape[1]
    merged = call(
        merge_kernel,
        (1,),
        [whole(w_gateup.shape), whole(w_down.shape)],
        whole((units // UNIT, 3 * depth, UNIT)),
        jax.ShapeDtypeStruct((units // UNIT, 3 * depth, UNIT), BF16),
        nbytes=12 * depth * units,
    )(following(info, head_parts[0]), w_gateup, w_down)
    weights = lax.all_gather(merged, "req", axis=0)

    shared = call(
        functools.partial(hidden_kernel, slots, nz, sizes),
        (1,),
        [whole((rows, width))],
        quarter_specs * 2,
        quarter_shapes * 2,
        vmem=20,
        flops=4 * sum(quarters) * rows * width,
        nbytes=2 * rows * width,
    )(following(info, head_parts[0]), hidden.reshape(rows, width))
    hidden_own = shared[:2]
    hidden_other = [lax.ppermute(piece, "req", swap) for piece in shared[2:]]

    parts = head_parts
    for s in range(2, nz):
        came = [reduce_step(parts[h], came[h], s, order, z, nz) for h in range(2)]
    streams, rights, lefts = [], [], []
    for h in range(2):
        q, spec = quarters[h], quarter_specs[h]
        terms = [lax.dynamic_index_in_dim(parts[h], z, 0, keepdims=False), *came[h]]
        stream, mid = call(
            stream_kernel,
            (1,),
            [spec] * 2 + [whole((1, width))] + [spec] * len(terms),
            [spec, spec],
            [quarter_shapes[h]] * 2,
            nbytes=14 * q * width,
        )(following(info, head_parts[1]), hidden_own[h], hidden_other[h], gain_mlp, *terms)
        streams.append(stream)
        rights.append([mid])
        lefts.append([mid])
        spread_step(rights[h], lefts[h], 1, order, z, nz)
    for s in range(2, nz):
        for h in range(2):
            spread_step(rights[h], lefts[h], s, order, z, nz)

    parts, came = [], []
    for h in range(2):
        q, size = quarters[h], sizes[h]
        part_shape = jax.ShapeDtypeStruct((nz, q, width), BF16)
        unit_parts = call(
            functools.partial(unit_kernel, nz),
            (units // UNIT,),
            [ANY] * (2 * nz - 1)
            + [pl.BlockSpec((n, 1) + weights.shape[2:], lambda b, _: (0, b, 0, 0))],
            whole(part_shape.shape),
            part_shape,
            [
                pltpu.VMEM((size, width), BF16),
                pltpu.VMEM((size, width), F32),
                pltpu.SemaphoreType.DMA((nz,)),
            ],
            vmem=28,
            flops=6 * size * width * units,
            nbytes=2 * weights.size,
        )(info, *rights[h], *lefts[h][1:], weights)
        parts.append(unit_parts)
        came.append(reduce_start(unit_parts, order, z, nz)[1])
    for s in range(2, nz):
        came = [reduce_step(parts[h], came[h], s, order, z, nz) for h in range(2)]

    sums, rights, lefts = [], [], []
    for h in range(2):
        q, size, spec = quarters[h], sizes[h], quarter_specs[h]
        terms = [lax.dynamic_index_in_dim(parts[h], z, 0, keepdims=False), *came[h]]
        extra = [(slots_all, width)] if h == 1 else []
        finished = call(
            functools.partial(finish_kernel, slots, size, h, len(terms)),
            (1,),
            [spec, whole((1, width))] + [spec] * len(terms),
            [spec, whole((8, 128))] + [whole(e) for e in extra],
            [quarter_shapes[h], jax.ShapeDtypeStruct((8, 128), F32)]
            + [jax.ShapeDtypeStruct(e, BF16) for e in extra],
            nbytes=10 * q * width,
        )(info, streams[h], final_gain, *terms)
        sums.append(finished[1])
        rights.append([finished[0]])
        lefts.append([finished[0]])
        spread_step(rights[h], lefts[h], 1, order, z, nz)
    every = finished[2]
    steps = list(hops(n, nz))

    def share(step):
        nonlocal every
        if step < len(steps):
            (message,) = order(every)
            every = every + lax.ppermute(message, *steps[step])

    share(0)
    done = 1
    for s in range(2, nz):
        for h in range(2):
            spread_step(rights[h], lefts[h], s, order, z, nz)
            if s < nz - 1:
                share(done)
                done += 1
    while done < len(steps):
        share(done)
        done += 1

    def ordered(h):
        size = sizes[h]
        rights[h][-1], lefts[h][-1], _ = lax.optimization_barrier(
            (rights[h][-1], lefts[h][-1], order.before)
        )
        mine = call(
            functools.partial(order_kernel, nz),
            (1,),
            [ANY] * (2 * nz - 1),
            whole((size, width)),
            jax.ShapeDtypeStruct((size, width), BF16),
            [pltpu.SemaphoreType.DMA((nz,))],
            nbytes=4 * size * width,
        )(info, *rights[h], *lefts[h][1:])
        (mine,) = order(mine)
        return mine, lax.ppermute(mine, "req", swap)

    def unpacked(h, mine, theirs, held):
        size = sizes[h]
        return call(
            functools.partial(unpack_kernel, slots, h),
            (slots,),
            [ANY, ANY] + [ANY] * len(held),
            pl.BlockSpec((half, width), lambda s, _, h=h: (2 * s + h, 0)),
            jax.ShapeDtypeStruct((rows, width), BF16),
            [pltpu.VMEM((2 * size + half, width), BF16), pltpu.SemaphoreType.DMA((2,))],
            nbytes=2 * rows * width,
            aliases={3: 0} if held else None,
        )(info, mine, theirs, *held)

    block = vocab.shape[0] // 3
    peaks = call(
        peak_kernel,
        (3,),
        [whole(every.shape), pl.BlockSpec((block, width), lambda b, _: (b, 0))],
        whole((8, 128)),
        jax.ShapeDtypeStruct((8, 128), F32),
        flops=2 * slots_all * vocab.size,
        nbytes=2 * vocab.size,
    )(info, every, vocab)
    both = jnp.concatenate([sums[0] + sums[1], peaks], axis=0)
    row = lax.broadcasted_iota(jnp.int32, both.shape, 0)

    def combine(both, hop):
        (message,) = order(both)
        arrived = lax.ppermute(message, *hop)
        return jnp.where(row < 8, both + arrived, jnp.maximum(both, arrived))

    early = ordered(0)
    late = ordered(1)
    out = unpacked(0, *early, [])
    for hop in steps:
        both = combine(both, hop)
    out = unpacked(1, *late, [out])
    return out.reshape(slots, length, width), both


def per_device(sizes_n, *arrays):
    (hidden, lengths, slot_request, adapter_of, adapter_slot, gain_attn, gain_mlp, final_gain) = (
        arrays[:8]
    )
    (w_qkv, w_out, w_gateup, w_down, adapter_down, adapter_up, vocab) = arrays[8:]
    n, nz = sizes_n
    slots, length, width = hidden.shape
    me, z = lax.axis_index("req"), lax.axis_index("mlp")
    part_rows = slots * length // 2
    classes = [
        (part_rows * a // 8, part_rows * b // 8 + c) for a, b, c in CLASSES
    ]
    factor_shape = (slots, adapter_down.shape[1], width + adapter_up.shape[2])
    info, *picked = pl.pallas_call(
        functools.partial(setup_kernel, slots, length // 2, classes),
        in_specs=[SMEM] * 6 + [pl.BlockSpec(memory_space=pltpu.VMEM)] * 2,
        out_specs=[SMEM] + [pl.BlockSpec(memory_space=pltpu.VMEM)] * n,
        out_shape=[jax.ShapeDtypeStruct((TABLES + 9 * slots,), jnp.int32)]
        + [jax.ShapeDtypeStruct(factor_shape, BF16)] * n,
        compiler_params=pltpu.CompilerParams(vmem_limit_bytes=60 * MIB),
    )(
        me.reshape(1), z.reshape(1), lengths, slot_request, adapter_of, adapter_slot,
        adapter_down, adapter_up,
    )
    operands = (
        info,
        hidden,
        tuple(g.reshape(1, width) for g in (gain_attn, gain_mlp, final_gain)),
        w_qkv.transpose(1, 0, 2),
        w_out,
        w_gateup,
        w_down,
        tuple(picked),
        vocab,
    )
    branches = [
        functools.partial(layer, sizes, sizes_n, adapter_down.shape[0]) for sizes in classes
    ]
    if len(branches) == 1:
        out, both = branches[0](*operands)
    else:
        out, both = lax.switch(info[CLASS], branches, *operands)
    slots_all = slot_request.shape[0]
    norm_sums, peaks = both[0, :slots_all], both[8, :slots_all]
    requests = jnp.arange(slots_all, dtype=jnp.int32)
    owners = slot_request[None, :] == requests[:, None]
    norm_sums = jnp.sum(jnp.where(owners, norm_sums[None, :], 0.0), axis=1)
    request_norm = jnp.sqrt(norm_sums / (lengths.astype(F32) * width))
    request_peak = jnp.sum(jnp.where(owners, peaks[None, :], 0.0), axis=1)
    return out, request_norm, request_peak


def solution(mesh):
    return jax.shard_map(
        functools.partial(per_device, (mesh.shape["req"], mesh.shape["mlp"])),
        mesh=mesh,
        in_specs=(
            P("req", None, None),
            P(),
            P(),
            P(),
            P(),
            P(),
            P(),
            P(),
            P(None, None, "mlp"),
            P("mlp", None),
            P("req", None, "mlp"),
            P("mlp", "req"),
            P("req", None, None),
            P("req", None, "mlp"),
            P(("req", "mlp"), None),
        ),
        out_specs=(P("req", None, None), P(), P()),
        check_vma=False,
    )
```

```python
import functools
import math

import jax
import jax.numpy as jnp
import numpy as np
from jax import lax
from jax.experimental import pallas as pl
from jax.experimental.pallas import tpu as pltpu
from jax.sharding import PartitionSpec as P

HEAD_WIDTH = 64
EPSILON = 1e-05
ROPE_BASE = 130000.0
ADAPTER_SCALE = 2.0
MASKED = -1e30
F32, BF16 = jnp.float32, jnp.bfloat16
UNIT = 256
CLASSES = [(7, 5, 0), (8, 5, 0), (8, 6, 0), (8, 8, 64)]
MIB = 1024 * 1024

ME, Z, CORE, CLASS, TABLES = 0, 1, 2, 3, 8
LAST_ROWS = 16
ANY = pl.BlockSpec(memory_space=pl.ANY)
SMEM = pl.BlockSpec(memory_space=pltpu.SMEM)


def nt(a, b):
    return lax.dot_general(a, b, (((1,), (1,)), ((), ())), preferred_element_type=F32)


def nn(a, b):
    return jnp.dot(a, b, preferred_element_type=F32)


def call(
    kernel, grid, ins, outs, shapes, scratch=(), flops=0, nbytes=0, aliases=None, vmem=16
):
    spec = pltpu.PrefetchScalarGridSpec(
        num_scalar_prefetch=1, grid=grid, in_specs=ins, out_specs=outs, scratch_shapes=scratch
    )
    return pl.pallas_call(
        kernel,
        grid_spec=spec,
        out_shape=shapes,
        input_output_aliases=aliases or {},
        compiler_params=pltpu.CompilerParams(vmem_limit_bytes=vmem * MIB),
        cost_estimate=pl.CostEstimate(
            flops=int(flops), bytes_accessed=int(nbytes), transcendentals=0
        ),
    )


def whole(shape):
    zeros = (0,) * len(shape)
    return pl.BlockSpec(tuple(shape), lambda *_: zeros)


def rope_tables(length):
    half = HEAD_WIDTH // 2
    frequency = np.float32(ROPE_BASE) ** (-(np.arange(half, dtype=np.float32) * 2.0 / HEAD_WIDTH))
    angles = np.arange(length, dtype=np.float32)[:, None] * frequency.astype(np.float32)[None, :]
    angles = angles.astype(np.float32)
    cosine, sine = np.cos(angles), np.sin(angles)
    return (
        np.concatenate([cosine] * 4, axis=1).astype(np.float32),
        np.concatenate([-sine, sine, -sine, sine], axis=1).astype(np.float32),
    )


def rotate(block, cosine, sine):
    lane = lax.broadcasted_iota(jnp.int32, block.shape, 1)
    front = (lane % HEAD_WIDTH) < HEAD_WIDTH // 2
    partner = jnp.where(
        front, pltpu.roll(block, 128 - HEAD_WIDTH // 2, 1), pltpu.roll(block, HEAD_WIDTH // 2, 1)
    )
    return block * cosine + partner * sine


def live_at(slots, h, g):
    return TABLES + slots + h * 4 * slots + g


def place_at(slots, h, g):
    return TABLES + slots + h * 4 * slots + 2 * slots + g


def setup_kernel(
    slots, half, classes, me_ref, z_ref, lengths, slot_request, adapter_of, adapter_slot, down, up,
    info, *outs
):
    table_rows, _, width = down.shape
    me, z = me_ref[0], z_ref[0]
    core, chip = lax.rem(me, 2), lax.div(me, 2)
    chip_slots = 2 * slots
    info[ME], info[Z], info[CORE] = me, z, core

    def split(slot):
        live = lengths[slot_request[slot]]
        first = jnp.minimum(live, half)
        return first, live - first

    def aligned(live):
        return lax.div(live + 15, 16) * 16

    most = [jnp.int32(0), jnp.int32(0)]
    for c in range(slot_request.shape[0] // chip_slots):
        total = [jnp.int32(0), jnp.int32(LAST_ROWS)]
        for g in range(chip_slots):
            for h, live in enumerate(split(c * chip_slots + g)):
                total[h] = total[h] + aligned(live)
        most = [jnp.maximum(most[h], total[h]) for h in range(2)]
    choice = jnp.int32(len(classes) - 1)
    for i in reversed(range(len(classes) - 1)):
        fits = (most[0] <= 2 * classes[i][0]) & (most[1] <= 2 * classes[i][1])
        choice = jnp.where(fits, i, choice)
    info[CLASS] = choice
    total = [jnp.int32(0), jnp.int32(LAST_ROWS)]
    for g in range(chip_slots):
        for h, live in enumerate(split(chip * chip_slots + g)):
            info[live_at(slots, h, g)] = live
            info[place_at(slots, h, g)] = total[h]
            total[h] = total[h] + aligned(live)
    for s in range(slots):
        info[TABLES + s] = adapter_slot[adapter_of[slot_request[me * slots + s]]]
    for j, out in enumerate(outs):
        for s in range(slots):
            slot = (me ^ j) * slots + s
            row = lax.rem(adapter_slot[adapter_of[slot_request[slot]]], table_rows)
            out[s, :, :width] = down[row]
            out[s, :, width:] = up[row]


def merge_kernel(info, gate_up, down, out):
    depth, units = down.shape[1], down.shape[0]
    for b in range(units // UNIT):
        at = slice(b * UNIT, (b + 1) * UNIT)
        out[b, 0:depth] = gate_up[:, 0, at]
        out[b, depth : 2 * depth] = gate_up[:, 1, at]
        out[b, 2 * depth :] = down[at, :] if depth == UNIT else down[at, :].T


def project_kernel(
    info, x_ref, gain_ref, w_ref, cos_ref, sin_ref, k_ref, v_ref, q_ref, normed_ref
):
    slots, rows, width = x_ref.shape
    group = 64
    for s in range(slots):
        for i in range(rows // group):
            x = x_ref[s, i * group : (i + 1) * group].astype(F32)
            mean = jnp.mean(x * x, axis=-1, keepdims=True)
            at = slice(s * rows + i * group, s * rows + (i + 1) * group)
            normed_ref[at] = (x * lax.rsqrt(mean + EPSILON) * gain_ref[...]).astype(BF16)
    product = nn(normed_ref[...], w_ref[1])
    for s in range(slots):
        at = slice(s * rows, (s + 1) * rows)
        for g in range(product.shape[1] // 128):
            lanes = slice(g * 128, g * 128 + 128)
            k_ref[at, lanes] = rotate(product[at, lanes], cos_ref[...], sin_ref[...]).astype(BF16)
    v_ref[...] = nn(normed_ref[...], w_ref[2]).astype(BF16)
    q_ref[...] = nn(normed_ref[...], w_ref[0])


def attend_kernel(slots, table_rows, n, h, info, q_ref, normed_ref, cos_ref, sin_ref, *rest):
    keys, values = rest[: h + 1], rest[h + 1 : 2 * h + 2]
    received, (out_ref, queries) = rest[2 * h + 2 : 2 * h + 2 + (n if h == 0 else 1)], rest[-2:]
    s = pl.program_id(0)
    length, columns = q_ref.shape
    width = normed_ref.shape[1]
    if h == 0:
        out_ref, picked, queries, sem = rest[-4:]
        factors = picked.at[0]
        source = info[ME] ^ lax.div(info[TABLES + s], table_rows)
        for j in range(n):

            @pl.when(source == j)
            def _(j=j):
                pltpu.make_async_copy(received[j].at[s], factors, sem.at[0]).start()

        pltpu.make_async_copy(received[0].at[s], factors, sem.at[0]).wait()
    else:
        factors = received[0].at[0]
    low_rank = nt(normed_ref[...], factors[:, :width]).astype(BF16)
    raised = nn(low_rank, factors[:, width:])
    full = q_ref[...] + ADAPTER_SCALE * raised
    for g in range(columns // 128):
        lanes = slice(g * 128, g * 128 + 128)
        queries[:, lanes] = rotate(full[:, lanes], cos_ref[...], sin_ref[...]).astype(BF16)
    step = length
    scale = HEAD_WIDTH ** (-0.5) * math.log2(math.e)

    def pair(g):
        lanes = slice(g * 128, g * 128 + 128)
        for b in range(length // step):
            end = (b + 1) * step
            q = queries[b * step : end, lanes]
            first = lax.broadcasted_iota(jnp.int32, q.shape, 1) < HEAD_WIDTH
            zero = jnp.zeros_like(q)
            both = jnp.concatenate([jnp.where(first, q, zero), jnp.where(first, zero, q)], axis=0)
            scores = nt(both, keys[h][0:end, lanes]) * scale
            row = lax.broadcasted_iota(jnp.int32, scores.shape, 0) % step + b * step
            col = lax.broadcasted_iota(jnp.int32, scores.shape, 1)
            scores = [jnp.where(col <= row, scores, MASKED)]
            used = [values[h][0:end, lanes]]
            for before in range(h):
                scores.append(nt(both, keys[before][:, lanes]) * scale)
                used.append(values[before][:, lanes])
            top = functools.reduce(
                jnp.maximum, [jnp.max(part, axis=1, keepdims=True) for part in scores]
            )
            weights = [jnp.exp2(part - top) for part in scores]
            total = sum(jnp.sum(part, axis=1, keepdims=True) for part in weights)
            mixed = sum(nn(part.astype(BF16), value) for part, value in zip(weights, used))
            mixed = mixed / total
            out_ref[b * step : end, lanes] = jnp.where(first, mixed[:step], mixed[step:]).astype(
                BF16
            )

    for g in range(columns // 128):
        pair(g)


def targets(info, row, slots, h, half, core, stride, start):
    place = jnp.full(row.shape, -1, jnp.int32)
    for s in range(slots):
        g = core * slots + s
        live = info[live_at(slots, h, g)]
        at = info[place_at(slots, h, g)]
        inside = (row >= at) & (row < at + live)
        place = jnp.where(inside, row - at + s * stride + start, place)
    return place


def last_targets(info, row, slots, half, core, h, stride, start):
    place = jnp.full(row.shape, -1, jnp.int32)
    for s in range(slots):
        g = core * slots + s
        second = info[live_at(slots, 1, g)]
        live = info[live_at(slots, 0, g)] if h == 0 else second
        there = (second > 0) if h == 1 else (second == 0)
        place = jnp.where((row == g) & there, s * stride + start + live - 1, place)
    return place


def one_hot(place, columns):
    col = lax.broadcasted_iota(jnp.int32, (place.shape[0], columns), 1)
    return jnp.where(col == place, 1.0, 0.0).astype(BF16)


def hidden_kernel(slots, nz, sizes, info, hidden_ref, *outs):
    count = len(sizes)
    tokens = hidden_ref.shape[0]
    length = tokens // slots
    half = length // 2
    core = info[CORE]
    for h in range(count):
        quarter = sizes[h] // nz
        for whose in range(2):
            target_core = core if whose == 0 else 1 - core
            base = target_core * sizes[h] + info[Z] * quarter
            row = lax.broadcasted_iota(jnp.int32, (quarter, 1), 0) + base
            place = targets(info, row, slots, h, half, core, length, h * half)
            if h == 1:
                for part in range(2):
                    late = last_targets(info, row, slots, half, core, part, length, part * half)
                    place = jnp.maximum(place, late)
            outs[whose * count + h][...] = nn(one_hot(place, tokens), hidden_ref[...]).astype(BF16)


def mix_kernel(slots, size, h, info, w_ref, *rest):
    parts, out_ref = rest[:-1], rest[-1]
    tokens = parts[0].shape[0]
    half = tokens // slots
    core = info[CORE]
    cores = (core, 1 - core)
    row = lax.broadcasted_iota(jnp.int32, (size, 1), 0) + core * size
    packed = 0.0
    for whose in range(2):
        place = targets(info, row, slots, h, half, cores[whose], half, 0)
        if h == 1:
            late = last_targets(info, row, slots, half, cores[whose], 1, half, 0)
            place = jnp.maximum(place, late)
        packed = packed + nn(one_hot(place, tokens), parts[whose][...])
    if h == 1:
        front = 0.0
        for whose in range(2):
            place = last_targets(info, row[:LAST_ROWS], slots, half, cores[whose], 0, half, 0)
            front = front + nn(one_hot(place, tokens), parts[2 + whose][...])
        packed = jnp.concatenate([packed[:LAST_ROWS] + front, packed[LAST_ROWS:]], axis=0)
    product = nn(packed.astype(BF16), w_ref[...]).astype(BF16)
    out_ref[...] = product.reshape(out_ref.shape)


def stream_kernel(info, own, other, gain, *rest):
    terms, (stream_ref, normed_ref) = rest[:-2], rest[-2:]
    mixed = sum(term[...].astype(F32) for term in terms)
    hidden = own[...].astype(F32) + other[...].astype(F32)
    stream = (hidden + mixed).astype(BF16)
    stream_ref[...] = stream
    x = stream.astype(F32)
    mean = jnp.mean(x * x, axis=-1, keepdims=True)
    normed_ref[...] = (x * lax.rsqrt(mean + EPSILON) * gain[...]).astype(BF16)


def finish_kernel(slots, size, h, count, info, stream, gain, *rest):
    terms, (out_ref, sums_ref), lasts = rest[:count], rest[count : count + 2], rest[count + 2 :]
    quarter, width = stream.shape
    chip_slots = 2 * slots
    total = sum(term[...].astype(F32) for term in terms)
    result = stream[...].astype(F32) + total
    base = info[CORE] * size + info[Z] * quarter
    row = lax.broadcasted_iota(jnp.int32, (quarter, 1), 0) + base
    keep = (row < chip_slots) if h == 1 else (row < 0)
    belongs = []
    for g in range(chip_slots):
        live, at = info[live_at(slots, h, g)], info[place_at(slots, h, g)]
        inside = (row >= at) & (row < at + live)
        belongs.append(inside)
        keep = keep | inside
    rounded = jnp.where(keep, result, 0.0).astype(BF16)
    out_ref[...] = rounded
    wide = rounded.astype(F32)
    squares = jnp.sum(wide * wide, axis=1, keepdims=True)
    lane = lax.broadcasted_iota(jnp.int32, sums_ref.shape, 1)
    first_slot = lax.div(info[ME], 2) * chip_slots
    sums = jnp.zeros(sums_ref.shape, F32)
    for g in range(chip_slots):
        part = jnp.sum(jnp.where(belongs[g], squares, 0.0))
        sums = jnp.where(lane == first_slot + g, part, sums)
    sums_ref[...] = sums
    for last_ref in lasts:
        last_ref[...] = jnp.zeros(last_ref.shape, BF16)
        front = wide[:LAST_ROWS]
        mean = jnp.mean(front * front, axis=-1, keepdims=True)
        last = (front * lax.rsqrt(mean + EPSILON) * gain[...]).astype(BF16)
        slot = lax.broadcasted_iota(jnp.int32, (last_ref.shape[0], LAST_ROWS), 0) - first_slot
        kept = lax.broadcasted_iota(jnp.int32, slot.shape, 1)
        pick = jnp.where((slot == kept) & (kept < chip_slots), 1.0, 0.0).astype(BF16)

        @pl.when(base == 0)
        def _():
            last_ref[...] = nn(pick, last).astype(BF16)


def in_order(nz, z, own, rights, lefts, out, sems):
    quarter = own.shape[0]

    def copy(piece, place):
        return pltpu.make_async_copy(
            piece, out.at[pl.ds(place * quarter, quarter)], sems.at[place]
        )

    for place in range(nz):

        @pl.when(z == place)
        def _(place=place):
            copy(own, place).start()

        for d in range(1, nz):

            @pl.when(z - place == d)
            def _(place=place, d=d):
                copy(rights[d - 1], place).start()

            @pl.when(place - z == d)
            def _(place=place, d=d):
                copy(lefts[d - 1], place).start()

    for place in range(nz):
        copy(own, place).wait()


def order_kernel(nz, info, own, *rest):
    rights, lefts, (out, sems) = rest[: nz - 1], rest[nz - 1 : 2 * nz - 2], rest[2 * nz - 2 :]
    in_order(nz, info[Z], own, rights, lefts, out, sems)


def unpack_kernel(slots, h, info, mine, theirs, *rest):
    out, packed, sems = rest[-3:]
    s = pl.program_id(0)
    size = mine.shape[0]
    core = info[CORE]

    @pl.when(s == 0)
    def _():
        copies = [
            pltpu.make_async_copy(
                piece,
                packed.at[pl.ds(pl.multiple_of(place * size, 16), size)],
                sems.at[i],
            )
            for i, (piece, place) in enumerate(((mine, core), (theirs, 1 - core)))
        ]
        for copy in copies:
            copy.start()
        for copy in copies:
            copy.wait()

    g = core * slots + s
    live, at = info[live_at(slots, h, g)], info[place_at(slots, h, g)]
    rows = packed[pl.ds(pl.multiple_of(at, 16), out.shape[0])]
    row = lax.broadcasted_iota(jnp.int32, (out.shape[0], 1), 0)
    out[...] = jnp.where(row < live, rows, jnp.zeros((), BF16))


def unit_kernel(nz, info, own, *rest):
    rights, lefts = rest[: nz - 1], rest[nz - 1 : 2 * nz - 2]
    w_ref, out_ref, x, acc, sems = rest[2 * nz - 2 :]
    b = pl.program_id(0)
    n, _, depth, columns = w_ref.shape
    depth = depth // 3
    width = x.shape[1]

    @pl.when(b == 0)
    def _():
        in_order(nz, info[Z], own, rights, lefts, x, sems)
        acc[...] = jnp.zeros(acc.shape, F32)

    gate = nn(x[...], w_ref[:, 0, 0:depth].reshape(width, columns))
    up = nn(x[...], w_ref[:, 0, depth : 2 * depth].reshape(width, columns))
    active = (gate / (1.0 + jnp.exp(-gate)) * up).astype(BF16)
    if depth == UNIT:
        for r in range(n):
            at = slice(r * depth, (r + 1) * depth)
            acc[:, at] += nn(active, w_ref[r, 0, 2 * depth :])
    else:
        acc[...] += nt(active, w_ref[:, 0, 2 * depth :].reshape(width, columns))

    @pl.when(b == pl.num_programs(0) - 1)
    def _():
        out_ref[...] = acc[...].astype(BF16).reshape(out_ref.shape)


def peak_kernel(info, every, vocab, out):
    b = pl.program_id(0)
    best = jnp.max(nt(vocab[...], every[...]), axis=0, keepdims=True)
    best = jnp.broadcast_to(best, (out.shape[0], every.shape[0]))

    @pl.when(b == 0)
    def _():
        out[...] = jnp.zeros(out.shape, F32)
        out[:, : every.shape[0]] = best

    @pl.when(b > 0)
    def _():
        out[:, : every.shape[0]] = jnp.maximum(out[:, : every.shape[0]], best)


def following(info, array):
    return lax.optimization_barrier((info, array))[0]


class Order:
    def __init__(self):
        self.before = None

    def __call__(self, *arrays):
        if self.before is not None:
            *arrays, _ = lax.optimization_barrier((*arrays, self.before))
        elif len(arrays) > 1:
            arrays = lax.optimization_barrier(arrays)
        self.before = arrays[0]
        return arrays


def reduce_start(parts, order, z, nz):
    last = nz - 1
    index = jnp.where(z == 0, last, 0)
    (message,) = order(lax.dynamic_index_in_dim(parts, index, 0, keepdims=False))
    came = lax.ppermute(message, "mlp", [(0, 1), (last, last - 1)])
    return message, [came, came]


def reduce_step(parts, came, s, order, z, nz):
    def take(index):
        return lax.dynamic_index_in_dim(parts, jnp.clip(index, 0, nz - 1), 0, keepdims=False)

    last = nz - 1
    *came, _ = lax.optimization_barrier((*came, order.before))
    right, left = take(nz - s + z), take(s + z - nz)
    if s == 2:
        right = jnp.where(z == 0, right, right + came[0])
        left = jnp.where(z == last, left, left + came[1])
    else:
        right, left = right + came[0], left + came[1]
    right, left = order(right, left)
    return [
        lax.ppermute(right, "mlp", [(i, i + 1) for i in range(s)]),
        lax.ppermute(left, "mlp", [(last - i, last - 1 - i) for i in range(s)]),
    ]


def spread_step(rights, lefts, s, order, z, nz):
    last = nz - 1
    if s < last:
        right, left = order(rights[-1], lefts[-1])
        rights.append(lax.ppermute(right, "mlp", [(i, i + 1) for i in range(s - 1, last)]))
        lefts.append(lax.ppermute(left, "mlp", [(i + 1, i) for i in range(0, nz - s)]))
    else:
        (message,) = order(jnp.where(z == last - 1, rights[-1], lefts[-1]))
        message = lax.ppermute(message, "mlp", [(last - 1, last), (1, 0)])
        rights.append(message)
        lefts.append(message)


def hops(n, nz):
    bit = 2
    while bit < n * nz:
        if bit < n:
            yield "req", [(i, i ^ bit) for i in range(n)]
        else:
            yield "mlp", [(i, i ^ (bit // n)) for i in range(nz)]
        bit *= 2
    yield "req", [(i, i ^ 1) for i in range(n)]


def layer(sizes, sizes_n, table_rows, lengths, slot_request, info, hidden, gains, w_qkv, w_out, w_gateup, w_down, picked, vocab):
    n, nz = sizes_n
    z = lax.axis_index("mlp")
    gain_attn, gain_mlp, final_gain = gains
    slots, length, width = hidden.shape
    rows, half = slots * length, length // 2
    columns = w_qkv.shape[2]
    units = w_down.shape[0]
    slots_all = n * slots
    swap = [(i, i ^ 1) for i in range(n)]
    factor_shape = picked[0].shape
    received = [picked[0]] + [
        lax.ppermute(picked[j], "req", [(i, i ^ j) for i in range(n)]) for j in range(1, n)
    ]

    cosine, sine = rope_tables(length)
    part_rows = slots * half
    projected = []
    for h in range(2):
        table = pl.BlockSpec((half, 128), lambda i, _, h=h: (h, 0))
        projected.append(
            call(
                project_kernel,
                (1,),
                [
                    pl.BlockSpec((slots, half, width), lambda i, _, h=h: (0, h, 0)),
                    whole((1, width)),
                    whole(w_qkv.shape),
                    table,
                    table,
                ],
                [whole((part_rows, columns))] * 3 + [whole((part_rows, width))],
                [
                    jax.ShapeDtypeStruct((part_rows, columns), BF16),
                    jax.ShapeDtypeStruct((part_rows, columns), BF16),
                    jax.ShapeDtypeStruct((part_rows, columns), F32),
                    jax.ShapeDtypeStruct((part_rows, width), BF16),
                ],
                vmem=32,
                flops=2 * part_rows * width * 3 * columns,
                nbytes=2 * (2 * part_rows * width + 3 * width * columns),
            )(info, hidden, gain_attn, w_qkv, cosine, sine)
        )

    quarters = [size // nz for size in sizes]
    quarter_shapes = [jax.ShapeDtypeStruct((q, width), BF16) for q in quarters]
    quarter_specs = [whole((q, width)) for q in quarters]
    attended, other, head_parts, came, order = [], [], [], [], Order()
    for h in range(2):
        by_slot = lambda w: pl.BlockSpec((half, w), lambda s, _: (s, 0))
        table = pl.BlockSpec((half, 128), lambda s, _, h=h: (h, 0))
        by_factor = pl.BlockSpec((1,) + factor_shape[1:], lambda s, _: (s, 0, 0))
        own_factors = h == 0
        mixed = call(
            functools.partial(attend_kernel, slots, table_rows, n, h),
            (slots,),
            [by_slot(columns), by_slot(width), table, table]
            + [by_slot(columns)] * (2 * h + 2)
            + ([ANY] * n if own_factors else [by_factor]),
            [by_slot(columns)] + [by_factor] * own_factors,
            [jax.ShapeDtypeStruct((part_rows, columns), BF16)]
            + [jax.ShapeDtypeStruct(factor_shape, BF16)] * own_factors,
            [pltpu.VMEM((half, columns), BF16)] + [pltpu.SemaphoreType.DMA((1,))] * own_factors,
            flops=8 * part_rows * (h + 1) * half * columns,
            nbytes=2 * part_rows * (width + 6 * columns),
        )(
            following(info, projected[1][1] if own_factors else first),
            projected[h][2],
            projected[h][3],
            cosine,
            sine,
            *[projected[i][0] for i in range(h + 1)],
            *[projected[i][1] for i in range(h + 1)],
            *received,
        )
        attended.append(mixed[0])
        if own_factors:
            received = mixed[1:]
        other.append(lax.ppermute(attended[h], "req", swap))
        size, q = sizes[h], quarters[h]
        part_shape = jax.ShapeDtypeStruct((nz, q, width), BF16)
        parts = [attended[h], other[h]] + ([attended[0], other[0]] if h == 1 else [])
        mixed = call(
            functools.partial(mix_kernel, slots, size, h),
            (1,),
            [whole(w_out.shape)] + [whole((part_rows, columns))] * len(parts),
            whole(part_shape.shape),
            part_shape,
            vmem=24,
            flops=2 * size * columns * (2 * part_rows + width),
            nbytes=2 * (columns * (2 * part_rows + width) + size * width),
        )(info, w_out, *parts)
        head_parts.append(mixed)
        first, came_h = reduce_start(mixed, order, z, nz)
        came.append(came_h)

    depth = w_down.shape[1]
    merged = call(
        merge_kernel,
        (1,),
        [whole(w_gateup.shape), whole(w_down.shape)],
        whole((units // UNIT, 3 * depth, UNIT)),
        jax.ShapeDtypeStruct((units // UNIT, 3 * depth, UNIT), BF16),
        nbytes=12 * depth * units,
    )(following(info, head_parts[0]), w_gateup, w_down)
    weights = lax.all_gather(merged, "req", axis=0)

    shared = call(
        functools.partial(hidden_kernel, slots, nz, sizes),
        (1,),
        [whole((rows, width))],
        quarter_specs * 2,
        quarter_shapes * 2,
        vmem=20,
        flops=4 * sum(quarters) * rows * width,
        nbytes=2 * rows * width,
    )(following(info, head_parts[0]), hidden.reshape(rows, width))
    hidden_own = shared[:2]
    hidden_other = [lax.ppermute(piece, "req", swap) for piece in shared[2:]]

    parts = head_parts
    for s in range(2, nz):
        came = [reduce_step(parts[h], came[h], s, order, z, nz) for h in range(2)]
    streams, rights, lefts = [], [], []
    for h in range(2):
        q, spec = quarters[h], quarter_specs[h]
        terms = [lax.dynamic_index_in_dim(parts[h], z, 0, keepdims=False), *came[h]]
        stream, mid = call(
            stream_kernel,
            (1,),
            [spec] * 2 + [whole((1, width))] + [spec] * len(terms),
            [spec, spec],
            [quarter_shapes[h]] * 2,
            nbytes=14 * q * width,
        )(following(info, head_parts[1]), hidden_own[h], hidden_other[h], gain_mlp, *terms)
        streams.append(stream)
        rights.append([mid])
        lefts.append([mid])
        spread_step(rights[h], lefts[h], 1, order, z, nz)
    for s in range(2, nz):
        for h in range(2):
            spread_step(rights[h], lefts[h], s, order, z, nz)

    parts, came = [], []
    for h in range(2):
        q, size = quarters[h], sizes[h]
        part_shape = jax.ShapeDtypeStruct((nz, q, width), BF16)
        unit_parts = call(
            functools.partial(unit_kernel, nz),
            (units // UNIT,),
            [ANY] * (2 * nz - 1)
            + [pl.BlockSpec((n, 1) + weights.shape[2:], lambda b, _: (0, b, 0, 0))],
            whole(part_shape.shape),
            part_shape,
            [
                pltpu.VMEM((size, width), BF16),
                pltpu.VMEM((size, width), F32),
                pltpu.SemaphoreType.DMA((nz,)),
            ],
            vmem=28,
            flops=6 * size * width * units,
            nbytes=2 * weights.size,
        )(info, *rights[h], *lefts[h][1:], weights)
        parts.append(unit_parts)
        came.append(reduce_start(unit_parts, order, z, nz)[1])
    for s in range(2, nz):
        came = [reduce_step(parts[h], came[h], s, order, z, nz) for h in range(2)]

    sums, rights, lefts = [], [], []
    for h in range(2):
        q, size, spec = quarters[h], sizes[h], quarter_specs[h]
        terms = [lax.dynamic_index_in_dim(parts[h], z, 0, keepdims=False), *came[h]]
        extra = [(slots_all, width)] if h == 1 else []
        finished = call(
            functools.partial(finish_kernel, slots, size, h, len(terms)),
            (1,),
            [spec, whole((1, width))] + [spec] * len(terms),
            [spec, whole((8, 128))] + [whole(e) for e in extra],
            [quarter_shapes[h], jax.ShapeDtypeStruct((8, 128), F32)]
            + [jax.ShapeDtypeStruct(e, BF16) for e in extra],
            nbytes=10 * q * width,
        )(info, streams[h], final_gain, *terms)
        sums.append(finished[1])
        rights.append([finished[0]])
        lefts.append([finished[0]])
        spread_step(rights[h], lefts[h], 1, order, z, nz)
    every = finished[2]
    steps = list(hops(n, nz))

    def share(step):
        nonlocal every
        if step < len(steps):
            (message,) = order(every)
            every = every + lax.ppermute(message, *steps[step])

    share(0)
    done = 1
    for s in range(2, nz):
        for h in range(2):
            spread_step(rights[h], lefts[h], s, order, z, nz)
            if s < nz - 1:
                share(done)
                done += 1
    while done < len(steps):
        share(done)
        done += 1

    def ordered(h):
        size = sizes[h]
        rights[h][-1], lefts[h][-1], _ = lax.optimization_barrier(
            (rights[h][-1], lefts[h][-1], order.before)
        )
        mine = call(
            functools.partial(order_kernel, nz),
            (1,),
            [ANY] * (2 * nz - 1),
            whole((size, width)),
            jax.ShapeDtypeStruct((size, width), BF16),
            [pltpu.SemaphoreType.DMA((nz,))],
            nbytes=4 * size * width,
        )(info, *rights[h], *lefts[h][1:])
        (mine,) = order(mine)
        return mine, lax.ppermute(mine, "req", swap)

    def unpacked(h, mine, theirs, held):
        size = sizes[h]
        return call(
            functools.partial(unpack_kernel, slots, h),
            (slots,),
            [ANY, ANY] + [ANY] * len(held),
            pl.BlockSpec((half, width), lambda s, _, h=h: (2 * s + h, 0)),
            jax.ShapeDtypeStruct((rows, width), BF16),
            [pltpu.VMEM((2 * size + half, width), BF16), pltpu.SemaphoreType.DMA((2,))],
            nbytes=2 * rows * width,
            aliases={3: 0} if held else None,
        )(info, mine, theirs, *held)

    block = vocab.shape[0] // 3
    peaks = call(
        peak_kernel,
        (3,),
        [whole(every.shape), pl.BlockSpec((block, width), lambda b, _: (b, 0))],
        whole((8, 128)),
        jax.ShapeDtypeStruct((8, 128), F32),
        flops=2 * slots_all * vocab.size,
        nbytes=2 * vocab.size,
    )(info, every, vocab)
    both = jnp.concatenate([sums[0] + sums[1], peaks], axis=0)
    row = lax.broadcasted_iota(jnp.int32, both.shape, 0)

    def combine(both, hop):
        (message,) = order(both)
        arrived = lax.ppermute(message, *hop)
        return jnp.where(row < 8, both + arrived, jnp.maximum(both, arrived))

    early = ordered(0)
    late = ordered(1)
    out = unpacked(0, *early, [])
    for hop in steps:
        both = combine(both, hop)
    out = unpacked(1, *late, [out])
    norm_sums, peaks = both[0, :slots_all], both[8, :slots_all]
    requests = jnp.arange(slots_all, dtype=jnp.int32)
    owners = slot_request[None, :] == requests[:, None]
    norm_sums = jnp.sum(jnp.where(owners, norm_sums[None, :], 0.0), axis=1)
    request_norm = jnp.sqrt(norm_sums / (lengths.astype(F32) * width))
    request_peak = jnp.sum(jnp.where(owners, peaks[None, :], 0.0), axis=1)
    return out.reshape(slots, length, width), request_norm, request_peak


def per_device(sizes_n, *arrays):
    (hidden, lengths, slot_request, adapter_of, adapter_slot, gain_attn, gain_mlp, final_gain) = (
        arrays[:8]
    )
    (w_qkv, w_out, w_gateup, w_down, adapter_down, adapter_up, vocab) = arrays[8:]
    n, nz = sizes_n
    slots, length, width = hidden.shape
    me, z = lax.axis_index("req"), lax.axis_index("mlp")
    part_rows = slots * length // 2
    classes = [
        (part_rows * a // 8, part_rows * b // 8 + c) for a, b, c in CLASSES
    ]
    factor_shape = (slots, adapter_down.shape[1], width + adapter_up.shape[2])
    info, *picked = pl.pallas_call(
        functools.partial(setup_kernel, slots, length // 2, classes),
        in_specs=[SMEM] * 6 + [pl.BlockSpec(memory_space=pltpu.VMEM)] * 2,
        out_specs=[SMEM] + [pl.BlockSpec(memory_space=pltpu.VMEM)] * n,
        out_shape=[jax.ShapeDtypeStruct((TABLES + 9 * slots,), jnp.int32)]
        + [jax.ShapeDtypeStruct(factor_shape, BF16)] * n,
        compiler_params=pltpu.CompilerParams(vmem_limit_bytes=60 * MIB),
    )(
        me.reshape(1), z.reshape(1), lengths, slot_request, adapter_of, adapter_slot,
        adapter_down, adapter_up,
    )
    operands = (
        lengths,
        slot_request,
        info,
        hidden,
        tuple(g.reshape(1, width) for g in (gain_attn, gain_mlp, final_gain)),
        w_qkv.transpose(1, 0, 2),
        w_out,
        w_gateup,
        w_down,
        tuple(picked),
        vocab,
    )
    branches = [
        functools.partial(layer, sizes, sizes_n, adapter_down.shape[0]) for sizes in classes
    ]
    if len(branches) == 1:
        return branches[0](*operands)
    return lax.switch(info[CLASS], branches, *operands)


def solution(mesh):
    return jax.shard_map(
        functools.partial(per_device, (mesh.shape["req"], mesh.shape["mlp"])),
        mesh=mesh,
        in_specs=(
            P("req", None, None),
            P(),
            P(),
            P(),
            P(),
            P(),
            P(),
            P(),
            P(None, None, "mlp"),
            P("mlp", None),
            P("req", None, "mlp"),
            P("mlp", "req"),
            P("req", None, None),
            P("req", None, "mlp"),
            P(("req", "mlp"), None),
        ),
        out_specs=(P("req", None, None), P(), P()),
        check_vma=False,
    )
```

```python
import functools
import math

import jax
import jax.numpy as jnp
import numpy as np
from jax import lax
from jax.experimental import pallas as pl
from jax.experimental.pallas import tpu as pltpu
from jax.sharding import PartitionSpec as P

HEAD_WIDTH = 64
EPSILON = 1e-05
ROPE_BASE = 130000.0
ADAPTER_SCALE = 2.0
MASKED = -1e30
F32, BF16 = jnp.float32, jnp.bfloat16
UNIT = 256
CLASSES = [(7, 5, 0), (8, 5, 0), (8, 6, 0), (8, 8, 64)]
MIB = 1024 * 1024

ME, Z, CORE, CLASS, TABLES = 0, 1, 2, 3, 8
LAST_ROWS = 16
ANY = pl.BlockSpec(memory_space=pl.ANY)
SMEM = pl.BlockSpec(memory_space=pltpu.SMEM)


def nt(a, b):
    return lax.dot_general(a, b, (((1,), (1,)), ((), ())), preferred_element_type=F32)


def nn(a, b):
    return jnp.dot(a, b, preferred_element_type=F32)


def call(
    kernel, grid, ins, outs, shapes, scratch=(), flops=0, nbytes=0, aliases=None, vmem=12
):
    spec = pltpu.PrefetchScalarGridSpec(
        num_scalar_prefetch=1, grid=grid, in_specs=ins, out_specs=outs, scratch_shapes=scratch
    )
    return pl.pallas_call(
        kernel,
        grid_spec=spec,
        out_shape=shapes,
        input_output_aliases=aliases or {},
        compiler_params=pltpu.CompilerParams(vmem_limit_bytes=vmem * MIB),
        cost_estimate=pl.CostEstimate(
            flops=int(flops), bytes_accessed=int(nbytes), transcendentals=0
        ),
    )


def whole(shape):
    zeros = (0,) * len(shape)
    return pl.BlockSpec(tuple(shape), lambda *_: zeros)


def rope_tables(length):
    half = HEAD_WIDTH // 2
    frequency = np.float32(ROPE_BASE) ** (-(np.arange(half, dtype=np.float32) * 2.0 / HEAD_WIDTH))
    angles = np.arange(length, dtype=np.float32)[:, None] * frequency.astype(np.float32)[None, :]
    angles = angles.astype(np.float32)
    cosine, sine = np.cos(angles), np.sin(angles)
    return (
        np.concatenate([cosine] * 4, axis=1).astype(np.float32),
        np.concatenate([-sine, sine, -sine, sine], axis=1).astype(np.float32),
    )


def rotate(block, cosine, sine):
    lane = lax.broadcasted_iota(jnp.int32, block.shape, 1)
    front = (lane % HEAD_WIDTH) < HEAD_WIDTH // 2
    partner = jnp.where(
        front, pltpu.roll(block, 128 - HEAD_WIDTH // 2, 1), pltpu.roll(block, HEAD_WIDTH // 2, 1)
    )
    return block * cosine + partner * sine


def live_at(slots, h, g):
    return TABLES + slots + h * 4 * slots + g


def place_at(slots, h, g):
    return TABLES + slots + h * 4 * slots + 2 * slots + g


def setup_kernel(
    slots, half, classes, me_ref, z_ref, lengths, slot_request, adapter_of, adapter_slot, down, up,
    info, *outs
):
    table_rows, _, width = down.shape
    me, z = me_ref[0], z_ref[0]
    core, chip = lax.rem(me, 2), lax.div(me, 2)
    chip_slots = 2 * slots
    info[ME], info[Z], info[CORE] = me, z, core

    def split(slot):
        live = lengths[slot_request[slot]]
        first = jnp.minimum(live, half)
        return first, live - first

    def aligned(live):
        return lax.div(live + 15, 16) * 16

    most = [jnp.int32(0), jnp.int32(0)]
    for c in range(slot_request.shape[0] // chip_slots):
        total = [jnp.int32(0), jnp.int32(LAST_ROWS)]
        for g in range(chip_slots):
            for h, live in enumerate(split(c * chip_slots + g)):
                total[h] = total[h] + aligned(live)
        most = [jnp.maximum(most[h], total[h]) for h in range(2)]
    choice = jnp.int32(len(classes) - 1)
    for i in reversed(range(len(classes) - 1)):
        fits = (most[0] <= 2 * classes[i][0]) & (most[1] <= 2 * classes[i][1])
        choice = jnp.where(fits, i, choice)
    info[CLASS] = choice
    total = [jnp.int32(0), jnp.int32(LAST_ROWS)]
    for g in range(chip_slots):
        for h, live in enumerate(split(chip * chip_slots + g)):
            info[live_at(slots, h, g)] = live
            info[place_at(slots, h, g)] = total[h]
            total[h] = total[h] + aligned(live)
    for s in range(slots):
        info[TABLES + s] = adapter_slot[adapter_of[slot_request[me * slots + s]]]
    for j, out in enumerate(outs):
        for s in range(slots):
            slot = (me ^ j) * slots + s
            row = lax.rem(adapter_slot[adapter_of[slot_request[slot]]], table_rows)
            out[s, :, :width] = down[row]
            out[s, :, width:] = up[row]


def merge_kernel(info, gate_up, down, out):
    depth, units = down.shape[1], down.shape[0]
    for b in range(units // UNIT):
        at = slice(b * UNIT, (b + 1) * UNIT)
        out[b, 0:depth] = gate_up[:, 0, at]
        out[b, depth : 2 * depth] = gate_up[:, 1, at]
        out[b, 2 * depth :] = down[at, :] if depth == UNIT else down[at, :].T


def project_kernel(
    info, x_ref, gain_ref, w_ref, cos_ref, sin_ref, k_ref, v_ref, q_ref, normed_ref
):
    slots, rows, width = x_ref.shape
    group = 64
    for s in range(slots):
        for i in range(rows // group):
            x = x_ref[s, i * group : (i + 1) * group].astype(F32)
            mean = jnp.mean(x * x, axis=-1, keepdims=True)
            at = slice(s * rows + i * group, s * rows + (i + 1) * group)
            normed_ref[at] = (x * lax.rsqrt(mean + EPSILON) * gain_ref[...]).astype(BF16)
    product = nn(normed_ref[...], w_ref[1])
    for s in range(slots):
        at = slice(s * rows, (s + 1) * rows)
        for g in range(product.shape[1] // 128):
            lanes = slice(g * 128, g * 128 + 128)
            k_ref[at, lanes] = rotate(product[at, lanes], cos_ref[...], sin_ref[...]).astype(BF16)
    v_ref[...] = nn(normed_ref[...], w_ref[2]).astype(BF16)
    q_ref[...] = nn(normed_ref[...], w_ref[0])


def attend_kernel(slots, table_rows, n, h, info, q_ref, normed_ref, cos_ref, sin_ref, *rest):
    keys, values = rest[: h + 1], rest[h + 1 : 2 * h + 2]
    received, (out_ref, queries) = rest[2 * h + 2 : 2 * h + 2 + (n if h == 0 else 1)], rest[-2:]
    s = pl.program_id(0)
    length, columns = q_ref.shape
    width = normed_ref.shape[1]
    if h == 0:
        out_ref, picked, queries, sem = rest[-4:]
        factors = picked.at[0]
        source = info[ME] ^ lax.div(info[TABLES + s], table_rows)
        for j in range(n):

            @pl.when(source == j)
            def _(j=j):
                pltpu.make_async_copy(received[j].at[s], factors, sem.at[0]).start()

        pltpu.make_async_copy(received[0].at[s], factors, sem.at[0]).wait()
    else:
        factors = received[0].at[0]
    low_rank = nt(normed_ref[...], factors[:, :width]).astype(BF16)
    raised = nn(low_rank, factors[:, width:])
    full = q_ref[...] + ADAPTER_SCALE * raised
    for g in range(columns // 128):
        lanes = slice(g * 128, g * 128 + 128)
        queries[:, lanes] = rotate(full[:, lanes], cos_ref[...], sin_ref[...]).astype(BF16)
    step = length
    scale = HEAD_WIDTH ** (-0.5) * math.log2(math.e)

    def pair(g):
        lanes = slice(g * 128, g * 128 + 128)
        for b in range(length // step):
            end = (b + 1) * step
            q = queries[b * step : end, lanes]
            first = lax.broadcasted_iota(jnp.int32, q.shape, 1) < HEAD_WIDTH
            zero = jnp.zeros_like(q)
            both = jnp.concatenate([jnp.where(first, q, zero), jnp.where(first, zero, q)], axis=0)
            scores = nt(both, keys[h][0:end, lanes]) * scale
            row = lax.broadcasted_iota(jnp.int32, scores.shape, 0) % step + b * step
            col = lax.broadcasted_iota(jnp.int32, scores.shape, 1)
            scores = [jnp.where(col <= row, scores, MASKED)]
            used = [values[h][0:end, lanes]]
            for before in range(h):
                scores.append(nt(both, keys[before][:, lanes]) * scale)
                used.append(values[before][:, lanes])
            top = functools.reduce(
                jnp.maximum, [jnp.max(part, axis=1, keepdims=True) for part in scores]
            )
            weights = [jnp.exp2(part - top) for part in scores]
            total = sum(jnp.sum(part, axis=1, keepdims=True) for part in weights)
            mixed = sum(nn(part.astype(BF16), value) for part, value in zip(weights, used))
            mixed = mixed / total
            out_ref[b * step : end, lanes] = jnp.where(first, mixed[:step], mixed[step:]).astype(
                BF16
            )

    for g in range(columns // 128):
        pair(g)


def targets(info, row, slots, h, half, core, stride, start):
    place = jnp.full(row.shape, -1, jnp.int32)
    for s in range(slots):
        g = core * slots + s
        live = info[live_at(slots, h, g)]
        at = info[place_at(slots, h, g)]
        inside = (row >= at) & (row < at + live)
        place = jnp.where(inside, row - at + s * stride + start, place)
    return place


def last_targets(info, row, slots, half, core, h, stride, start):
    place = jnp.full(row.shape, -1, jnp.int32)
    for s in range(slots):
        g = core * slots + s
        second = info[live_at(slots, 1, g)]
        live = info[live_at(slots, 0, g)] if h == 0 else second
        there = (second > 0) if h == 1 else (second == 0)
        place = jnp.where((row == g) & there, s * stride + start + live - 1, place)
    return place


def one_hot(place, columns):
    col = lax.broadcasted_iota(jnp.int32, (place.shape[0], columns), 1)
    return jnp.where(col == place, 1.0, 0.0).astype(BF16)


def hidden_kernel(slots, nz, sizes, info, hidden_ref, *outs):
    count = len(sizes)
    tokens = hidden_ref.shape[0]
    length = tokens // slots
    half = length // 2
    core = info[CORE]
    for h in range(count):
        quarter = sizes[h] // nz
        for whose in range(2):
            target_core = core if whose == 0 else 1 - core
            base = target_core * sizes[h] + info[Z] * quarter
            row = lax.broadcasted_iota(jnp.int32, (quarter, 1), 0) + base
            place = targets(info, row, slots, h, half, core, length, h * half)
            if h == 1:
                for part in range(2):
                    late = last_targets(info, row, slots, half, core, part, length, part * half)
                    place = jnp.maximum(place, late)
            outs[whose * count + h][...] = nn(one_hot(place, tokens), hidden_ref[...]).astype(BF16)


def mix_kernel(slots, size, h, info, w_ref, *rest):
    parts, out_ref = rest[:-1], rest[-1]
    tokens = parts[0].shape[0]
    half = tokens // slots
    core = info[CORE]
    cores = (core, 1 - core)
    row = lax.broadcasted_iota(jnp.int32, (size, 1), 0) + core * size
    packed = 0.0
    for whose in range(2):
        place = targets(info, row, slots, h, half, cores[whose], half, 0)
        if h == 1:
            late = last_targets(info, row, slots, half, cores[whose], 1, half, 0)
            place = jnp.maximum(place, late)
        packed = packed + nn(one_hot(place, tokens), parts[whose][...])
    if h == 1:
        front = 0.0
        for whose in range(2):
            place = last_targets(info, row[:LAST_ROWS], slots, half, cores[whose], 0, half, 0)
            front = front + nn(one_hot(place, tokens), parts[2 + whose][...])
        packed = jnp.concatenate([packed[:LAST_ROWS] + front, packed[LAST_ROWS:]], axis=0)
    product = nn(packed.astype(BF16), w_ref[...]).astype(BF16)
    out_ref[...] = product.reshape(out_ref.shape)


def stream_kernel(info, own, other, gain, *rest):
    terms, (stream_ref, normed_ref) = rest[:-2], rest[-2:]
    mixed = sum(term[...].astype(F32) for term in terms)
    hidden = own[...].astype(F32) + other[...].astype(F32)
    stream = (hidden + mixed).astype(BF16)
    stream_ref[...] = stream
    x = stream.astype(F32)
    mean = jnp.mean(x * x, axis=-1, keepdims=True)
    normed_ref[...] = (x * lax.rsqrt(mean + EPSILON) * gain[...]).astype(BF16)


def finish_kernel(slots, size, h, count, info, stream, gain, *rest):
    terms, (out_ref, sums_ref), lasts = rest[:count], rest[count : count + 2], rest[count + 2 :]
    quarter, width = stream.shape
    chip_slots = 2 * slots
    total = sum(term[...].astype(F32) for term in terms)
    result = stream[...].astype(F32) + total
    base = info[CORE] * size + info[Z] * quarter
    row = lax.broadcasted_iota(jnp.int32, (quarter, 1), 0) + base
    keep = (row < chip_slots) if h == 1 else (row < 0)
    belongs = []
    for g in range(chip_slots):
        live, at = info[live_at(slots, h, g)], info[place_at(slots, h, g)]
        inside = (row >= at) & (row < at + live)
        belongs.append(inside)
        keep = keep | inside
    rounded = jnp.where(keep, result, 0.0).astype(BF16)
    out_ref[...] = rounded
    wide = rounded.astype(F32)
    squares = jnp.sum(wide * wide, axis=1, keepdims=True)
    lane = lax.broadcasted_iota(jnp.int32, sums_ref.shape, 1)
    first_slot = lax.div(info[ME], 2) * chip_slots
    sums = jnp.zeros(sums_ref.shape, F32)
    for g in range(chip_slots):
        part = jnp.sum(jnp.where(belongs[g], squares, 0.0))
        sums = jnp.where(lane == first_slot + g, part, sums)
    sums_ref[...] = sums
    for last_ref in lasts:
        last_ref[...] = jnp.zeros(last_ref.shape, BF16)
        front = wide[:LAST_ROWS]
        mean = jnp.mean(front * front, axis=-1, keepdims=True)
        last = (front * lax.rsqrt(mean + EPSILON) * gain[...]).astype(BF16)
        slot = lax.broadcasted_iota(jnp.int32, (last_ref.shape[0], LAST_ROWS), 0) - first_slot
        kept = lax.broadcasted_iota(jnp.int32, slot.shape, 1)
        pick = jnp.where((slot == kept) & (kept < chip_slots), 1.0, 0.0).astype(BF16)

        @pl.when(base == 0)
        def _():
            last_ref[...] = nn(pick, last).astype(BF16)


def in_order(nz, z, own, rights, lefts, out, sems):
    quarter = own.shape[0]

    def copy(piece, place):
        return pltpu.make_async_copy(
            piece, out.at[pl.ds(place * quarter, quarter)], sems.at[place]
        )

    for place in range(nz):

        @pl.when(z == place)
        def _(place=place):
            copy(own, place).start()

        for d in range(1, nz):

            @pl.when(z - place == d)
            def _(place=place, d=d):
                copy(rights[d - 1], place).start()

            @pl.when(place - z == d)
            def _(place=place, d=d):
                copy(lefts[d - 1], place).start()

    for place in range(nz):
        copy(own, place).wait()


def order_kernel(nz, info, own, *rest):
    rights, lefts, (out, sems) = rest[: nz - 1], rest[nz - 1 : 2 * nz - 2], rest[2 * nz - 2 :]
    in_order(nz, info[Z], own, rights, lefts, out, sems)


def unpack_kernel(slots, h, info, mine, theirs, *rest):
    out, packed, sems = rest[-3:]
    s = pl.program_id(0)
    size = mine.shape[0]
    core = info[CORE]

    @pl.when(s == 0)
    def _():
        copies = [
            pltpu.make_async_copy(
                piece,
                packed.at[pl.ds(pl.multiple_of(place * size, 16), size)],
                sems.at[i],
            )
            for i, (piece, place) in enumerate(((mine, core), (theirs, 1 - core)))
        ]
        for copy in copies:
            copy.start()
        for copy in copies:
            copy.wait()

    g = core * slots + s
    live, at = info[live_at(slots, h, g)], info[place_at(slots, h, g)]
    rows = packed[pl.ds(pl.multiple_of(at, 16), out.shape[0])]
    row = lax.broadcasted_iota(jnp.int32, (out.shape[0], 1), 0)
    out[...] = jnp.where(row < live, rows, jnp.zeros((), BF16))


def unit_kernel(nz, info, own, *rest):
    rights, lefts = rest[: nz - 1], rest[nz - 1 : 2 * nz - 2]
    w_ref, out_ref, x, acc, sems = rest[2 * nz - 2 :]
    b = pl.program_id(0)
    n, _, depth, columns = w_ref.shape
    depth = depth // 3
    width = x.shape[1]

    @pl.when(b == 0)
    def _():
        in_order(nz, info[Z], own, rights, lefts, x, sems)
        acc[...] = jnp.zeros(acc.shape, F32)

    gate = nn(x[...], w_ref[:, 0, 0:depth].reshape(width, columns))
    up = nn(x[...], w_ref[:, 0, depth : 2 * depth].reshape(width, columns))
    active = (gate / (1.0 + jnp.exp(-gate)) * up).astype(BF16)
    if depth == UNIT:
        for r in range(n):
            at = slice(r * depth, (r + 1) * depth)
            acc[:, at] += nn(active, w_ref[r, 0, 2 * depth :])
    else:
        acc[...] += nt(active, w_ref[:, 0, 2 * depth :].reshape(width, columns))

    @pl.when(b == pl.num_programs(0) - 1)
    def _():
        out_ref[...] = acc[...].astype(BF16).reshape(out_ref.shape)


def peak_kernel(info, every, vocab, out):
    b = pl.program_id(0)
    best = jnp.max(nt(vocab[...], every[...]), axis=0, keepdims=True)
    best = jnp.broadcast_to(best, (out.shape[0], every.shape[0]))

    @pl.when(b == 0)
    def _():
        out[...] = jnp.zeros(out.shape, F32)
        out[:, : every.shape[0]] = best

    @pl.when(b > 0)
    def _():
        out[:, : every.shape[0]] = jnp.maximum(out[:, : every.shape[0]], best)


def following(info, array):
    return lax.optimization_barrier((info, array))[0]


class Order:
    def __init__(self):
        self.before = None

    def __call__(self, *arrays):
        if self.before is not None:
            *arrays, _ = lax.optimization_barrier((*arrays, self.before))
        elif len(arrays) > 1:
            arrays = lax.optimization_barrier(arrays)
        self.before = arrays[0]
        return arrays


def reduce_start(parts, order, z, nz):
    last = nz - 1
    index = jnp.where(z == 0, last, 0)
    (message,) = order(lax.dynamic_index_in_dim(parts, index, 0, keepdims=False))
    came = lax.ppermute(message, "mlp", [(0, 1), (last, last - 1)])
    return message, [came, came]


def reduce_step(parts, came, s, order, z, nz):
    def take(index):
        return lax.dynamic_index_in_dim(parts, jnp.clip(index, 0, nz - 1), 0, keepdims=False)

    last = nz - 1
    *came, _ = lax.optimization_barrier((*came, order.before))
    right, left = take(nz - s + z), take(s + z - nz)
    if s == 2:
        right = jnp.where(z == 0, right, right + came[0])
        left = jnp.where(z == last, left, left + came[1])
    else:
        right, left = right + came[0], left + came[1]
    right, left = order(right, left)
    return [
        lax.ppermute(right, "mlp", [(i, i + 1) for i in range(s)]),
        lax.ppermute(left, "mlp", [(last - i, last - 1 - i) for i in range(s)]),
    ]


def spread_step(rights, lefts, s, order, z, nz):
    last = nz - 1
    if s < last:
        right, left = order(rights[-1], lefts[-1])
        rights.append(lax.ppermute(right, "mlp", [(i, i + 1) for i in range(s - 1, last)]))
        lefts.append(lax.ppermute(left, "mlp", [(i + 1, i) for i in range(0, nz - s)]))
    else:
        (message,) = order(jnp.where(z == last - 1, rights[-1], lefts[-1]))
        message = lax.ppermute(message, "mlp", [(last - 1, last), (1, 0)])
        rights.append(message)
        lefts.append(message)


def hops(n, nz):
    bit = 2
    while bit < n * nz:
        if bit < n:
            yield "req", [(i, i ^ bit) for i in range(n)]
        else:
            yield "mlp", [(i, i ^ (bit // n)) for i in range(nz)]
        bit *= 2
    yield "req", [(i, i ^ 1) for i in range(n)]


def layer(sizes, sizes_n, table_rows, lengths, slot_request, info, hidden, gains, w_qkv, w_out, w_gateup, w_down, picked, vocab):
    n, nz = sizes_n
    z = lax.axis_index("mlp")
    gain_attn, gain_mlp, final_gain = gains
    slots, length, width = hidden.shape
    rows, half = slots * length, length // 2
    columns = w_qkv.shape[2]
    units = w_down.shape[0]
    slots_all = n * slots
    swap = [(i, i ^ 1) for i in range(n)]
    factor_shape = picked[0].shape
    received = [picked[0]] + [
        lax.ppermute(picked[j], "req", [(i, i ^ j) for i in range(n)]) for j in range(1, n)
    ]

    cosine, sine = rope_tables(length)
    part_rows = slots * half
    projected = []
    for h in range(2):
        table = pl.BlockSpec((half, 128), lambda i, _, h=h: (h, 0))
        projected.append(
            call(
                project_kernel,
                (1,),
                [
                    pl.BlockSpec((slots, half, width), lambda i, _, h=h: (0, h, 0)),
                    whole((1, width)),
                    whole(w_qkv.shape),
                    table,
                    table,
                ],
                [whole((part_rows, columns))] * 3 + [whole((part_rows, width))],
                [
                    jax.ShapeDtypeStruct((part_rows, columns), BF16),
                    jax.ShapeDtypeStruct((part_rows, columns), BF16),
                    jax.ShapeDtypeStruct((part_rows, columns), F32),
                    jax.ShapeDtypeStruct((part_rows, width), BF16),
                ],
                vmem=26,
                flops=2 * part_rows * width * 3 * columns,
                nbytes=2 * (2 * part_rows * width + 3 * width * columns),
            )(info, hidden, gain_attn, w_qkv, cosine, sine)
        )

    quarters = [size // nz for size in sizes]
    quarter_shapes = [jax.ShapeDtypeStruct((q, width), BF16) for q in quarters]
    quarter_specs = [whole((q, width)) for q in quarters]
    attended, other, head_parts, came, order = [], [], [], [], Order()
    for h in range(2):
        by_slot = lambda w: pl.BlockSpec((half, w), lambda s, _: (s, 0))
        table = pl.BlockSpec((half, 128), lambda s, _, h=h: (h, 0))
        by_factor = pl.BlockSpec((1,) + factor_shape[1:], lambda s, _: (s, 0, 0))
        own_factors = h == 0
        mixed = call(
            functools.partial(attend_kernel, slots, table_rows, n, h),
            (slots,),
            [by_slot(columns), by_slot(width), table, table]
            + [by_slot(columns)] * (2 * h + 2)
            + ([ANY] * n if own_factors else [by_factor]),
            [by_slot(columns)] + [by_factor] * own_factors,
            [jax.ShapeDtypeStruct((part_rows, columns), BF16)]
            + [jax.ShapeDtypeStruct(factor_shape, BF16)] * own_factors,
            [pltpu.VMEM((half, columns), BF16)] + [pltpu.SemaphoreType.DMA((1,))] * own_factors,
            flops=8 * part_rows * (h + 1) * half * columns,
            nbytes=2 * part_rows * (width + 6 * columns),
        )(
            following(info, projected[1][1] if own_factors else first),
            projected[h][2],
            projected[h][3],
            cosine,
            sine,
            *[projected[i][0] for i in range(h + 1)],
            *[projected[i][1] for i in range(h + 1)],
            *received,
        )
        attended.append(mixed[0])
        if own_factors:
            received = mixed[1:]
        other.append(lax.ppermute(attended[h], "req", swap))
        size, q = sizes[h], quarters[h]
        part_shape = jax.ShapeDtypeStruct((nz, q, width), BF16)
        parts = [attended[h], other[h]] + ([attended[0], other[0]] if h == 1 else [])
        mixed = call(
            functools.partial(mix_kernel, slots, size, h),
            (1,),
            [whole(w_out.shape)] + [whole((part_rows, columns))] * len(parts),
            whole(part_shape.shape),
            part_shape,
            vmem=18,
            flops=2 * size * columns * (2 * part_rows + width),
            nbytes=2 * (columns * (2 * part_rows + width) + size * width),
        )(info, w_out, *parts)
        head_parts.append(mixed)
        first, came_h = reduce_start(mixed, order, z, nz)
        came.append(came_h)

    depth = w_down.shape[1]
    merged = call(
        merge_kernel,
        (1,),
        [whole(w_gateup.shape), whole(w_down.shape)],
        whole((units // UNIT, 3 * depth, UNIT)),
        jax.ShapeDtypeStruct((units // UNIT, 3 * depth, UNIT), BF16),
        nbytes=12 * depth * units,
    )(following(info, head_parts[0]), w_gateup, w_down)
    weights = lax.all_gather(merged, "req", axis=0)

    shared = call(
        functools.partial(hidden_kernel, slots, nz, sizes),
        (1,),
        [whole((rows, width))],
        quarter_specs * 2,
        quarter_shapes * 2,
        vmem=16,
        flops=4 * sum(quarters) * rows * width,
        nbytes=2 * rows * width,
    )(following(info, head_parts[0]), hidden.reshape(rows, width))
    hidden_own = shared[:2]
    hidden_other = [lax.ppermute(piece, "req", swap) for piece in shared[2:]]

    parts = head_parts
    for s in range(2, nz):
        came = [reduce_step(parts[h], came[h], s, order, z, nz) for h in range(2)]
    streams, rights, lefts = [], [], []
    for h in range(2):
        q, spec = quarters[h], quarter_specs[h]
        terms = [lax.dynamic_index_in_dim(parts[h], z, 0, keepdims=False), *came[h]]
        stream, mid = call(
            stream_kernel,
            (1,),
            [spec] * 2 + [whole((1, width))] + [spec] * len(terms),
            [spec, spec],
            [quarter_shapes[h]] * 2,
            nbytes=14 * q * width,
        )(
            following(info, head_parts[1] if h == 0 else weights),
            hidden_own[h],
            hidden_other[h],
            gain_mlp,
            *terms,
        )
        streams.append(stream)
        rights.append([mid])
        lefts.append([mid])
        spread_step(rights[h], lefts[h], 1, order, z, nz)
    for s in range(2, nz):
        for h in range(2):
            spread_step(rights[h], lefts[h], s, order, z, nz)

    parts, came = [], []
    for h in range(2):
        q, size = quarters[h], sizes[h]
        part_shape = jax.ShapeDtypeStruct((nz, q, width), BF16)
        unit_parts = call(
            functools.partial(unit_kernel, nz),
            (units // UNIT,),
            [ANY] * (2 * nz - 1)
            + [pl.BlockSpec((n, 1) + weights.shape[2:], lambda b, _: (0, b, 0, 0))],
            whole(part_shape.shape),
            part_shape,
            [
                pltpu.VMEM((size, width), BF16),
                pltpu.VMEM((size, width), F32),
                pltpu.SemaphoreType.DMA((nz,)),
            ],
            vmem=24,
            flops=6 * size * width * units,
            nbytes=2 * weights.size,
        )(info, *rights[h], *lefts[h][1:], weights)
        parts.append(unit_parts)
        came.append(reduce_start(unit_parts, order, z, nz)[1])
    for s in range(2, nz):
        came = [reduce_step(parts[h], came[h], s, order, z, nz) for h in range(2)]

    sums, rights, lefts = [], [], []
    for h in range(2):
        q, size, spec = quarters[h], sizes[h], quarter_specs[h]
        terms = [lax.dynamic_index_in_dim(parts[h], z, 0, keepdims=False), *came[h]]
        extra = [(slots_all, width)] if h == 1 else []
        finished = call(
            functools.partial(finish_kernel, slots, size, h, len(terms)),
            (1,),
            [spec, whole((1, width))] + [spec] * len(terms),
            [spec, whole((8, 128))] + [whole(e) for e in extra],
            [quarter_shapes[h], jax.ShapeDtypeStruct((8, 128), F32)]
            + [jax.ShapeDtypeStruct(e, BF16) for e in extra],
            nbytes=10 * q * width,
        )(info, streams[h], final_gain, *terms)
        sums.append(finished[1])
        rights.append([finished[0]])
        lefts.append([finished[0]])
        spread_step(rights[h], lefts[h], 1, order, z, nz)
    every = finished[2]
    steps = list(hops(n, nz))

    def share(step):
        nonlocal every
        if step < len(steps):
            (message,) = order(every)
            every = every + lax.ppermute(message, *steps[step])

    share(0)
    done = 1
    for s in range(2, nz):
        for h in range(2):
            spread_step(rights[h], lefts[h], s, order, z, nz)
            if s < nz - 1:
                share(done)
                done += 1
    while done < len(steps):
        share(done)
        done += 1

    def ordered(h):
        size = sizes[h]
        rights[h][-1], lefts[h][-1], _ = lax.optimization_barrier(
            (rights[h][-1], lefts[h][-1], order.before)
        )
        mine = call(
            functools.partial(order_kernel, nz),
            (1,),
            [ANY] * (2 * nz - 1),
            whole((size, width)),
            jax.ShapeDtypeStruct((size, width), BF16),
            [pltpu.SemaphoreType.DMA((nz,))],
            nbytes=4 * size * width,
        )(info, *rights[h], *lefts[h][1:])
        (mine,) = order(mine)
        return mine, lax.ppermute(mine, "req", swap)

    def unpacked(h, mine, theirs, held):
        size = sizes[h]
        return call(
            functools.partial(unpack_kernel, slots, h),
            (slots,),
            [ANY, ANY] + [ANY] * len(held),
            pl.BlockSpec((half, width), lambda s, _, h=h: (2 * s + h, 0)),
            jax.ShapeDtypeStruct((rows, width), BF16),
            [pltpu.VMEM((2 * size + half, width), BF16), pltpu.SemaphoreType.DMA((2,))],
            nbytes=2 * rows * width,
            aliases={3: 0} if held else None,
        )(info, mine, theirs, *held)

    block = vocab.shape[0] // 3
    peaks = call(
        peak_kernel,
        (3,),
        [whole(every.shape), pl.BlockSpec((block, width), lambda b, _: (b, 0))],
        whole((8, 128)),
        jax.ShapeDtypeStruct((8, 128), F32),
        flops=2 * slots_all * vocab.size,
        nbytes=2 * vocab.size,
    )(info, every, vocab)
    both = jnp.concatenate([sums[0] + sums[1], peaks], axis=0)
    row = lax.broadcasted_iota(jnp.int32, both.shape, 0)

    def combine(both, hop):
        (message,) = order(both)
        arrived = lax.ppermute(message, *hop)
        return jnp.where(row < 8, both + arrived, jnp.maximum(both, arrived))

    early = ordered(0)
    late = ordered(1)
    out = unpacked(0, *early, [])
    for hop in steps:
        both = combine(both, hop)
    out = unpacked(1, *late, [out])
    norm_sums, peaks = both[0, :slots_all], both[8, :slots_all]
    requests = jnp.arange(slots_all, dtype=jnp.int32)
    owners = slot_request[None, :] == requests[:, None]
    norm_sums = jnp.sum(jnp.where(owners, norm_sums[None, :], 0.0), axis=1)
    request_norm = jnp.sqrt(norm_sums / (lengths.astype(F32) * width))
    request_peak = jnp.sum(jnp.where(owners, peaks[None, :], 0.0), axis=1)
    return out.reshape(slots, length, width), request_norm, request_peak


def per_device(sizes_n, *arrays):
    (hidden, lengths, slot_request, adapter_of, adapter_slot, gain_attn, gain_mlp, final_gain) = (
        arrays[:8]
    )
    (w_qkv, w_out, w_gateup, w_down, adapter_down, adapter_up, vocab) = arrays[8:]
    n, nz = sizes_n
    slots, length, width = hidden.shape
    me, z = lax.axis_index("req"), lax.axis_index("mlp")
    part_rows = slots * length // 2
    classes = [
        (part_rows * a // 8, part_rows * b // 8 + c) for a, b, c in CLASSES
    ]
    factor_shape = (slots, adapter_down.shape[1], width + adapter_up.shape[2])
    info, *picked = pl.pallas_call(
        functools.partial(setup_kernel, slots, length // 2, classes),
        in_specs=[SMEM] * 6 + [pl.BlockSpec(memory_space=pltpu.VMEM)] * 2,
        out_specs=[SMEM] + [pl.BlockSpec(memory_space=pltpu.VMEM)] * n,
        out_shape=[jax.ShapeDtypeStruct((TABLES + 9 * slots,), jnp.int32)]
        + [jax.ShapeDtypeStruct(factor_shape, BF16)] * n,
        compiler_params=pltpu.CompilerParams(vmem_limit_bytes=60 * MIB),
    )(
        me.reshape(1), z.reshape(1), lengths, slot_request, adapter_of, adapter_slot,
        adapter_down, adapter_up,
    )
    operands = (
        lengths,
        slot_request,
        info,
        hidden,
        tuple(g.reshape(1, width) for g in (gain_attn, gain_mlp, final_gain)),
        w_qkv.transpose(1, 0, 2),
        w_out,
        w_gateup,
        w_down,
        tuple(picked),
        vocab,
    )
    branches = [
        functools.partial(layer, sizes, sizes_n, adapter_down.shape[0]) for sizes in classes
    ]
    if len(branches) == 1:
        return branches[0](*operands)
    index = (info[CLASS] + 1) % len(branches)
    return lax.switch(index, branches[-1:] + branches[:-1], *operands)


def solution(mesh):
    return jax.shard_map(
        functools.partial(per_device, (mesh.shape["req"], mesh.shape["mlp"])),
        mesh=mesh,
        in_specs=(
            P("req", None, None),
            P(),
            P(),
            P(),
            P(),
            P(),
            P(),
            P(),
            P(None, None, "mlp"),
            P("mlp", None),
            P("req", None, "mlp"),
            P("mlp", "req"),
            P("req", None, None),
            P("req", None, "mlp"),
            P(("req", "mlp"), None),
        ),
        out_specs=(P("req", None, None), P(), P()),
        check_vma=False,
    )
```
